128 devices in a mesh: rb: 16 (over z, y_lo, core), cb: 8 (over x, y_hi).
Axes of the slice: x: 4, y: 4 (y_hi: 2, y_lo: 2; y = y_hi * 2 + y_lo), z: 4, core: 2. Of those that a mesh axis runs over, the one named last changes fastest.
Arguments:
- pair_map: float32 [512, 512, 128], P(('rb', 'cb')), may hold values from -6 to 6
- norm_gain_start: float32 [128], replicated, may hold values from 0.1 to 1.9
- norm_shift_start: float32 [128], replicated, may hold values from -3 to 3
- proj_start: bfloat16 [128, 512], replicated, may hold values from -16 to 16
- bias_weight_start: bfloat16 [128, 4], replicated, may hold values from -1 to 1
- gate_bias_start: float32 [128], replicated, may hold values from -4 to 4
- out_weight_start: bfloat16 [128, 128], replicated, may hold values from -0.5 to 0.5
- out_bias_start: float32 [128], replicated, may hold values from -3 to 3
- norm_gain_end: float32 [128], replicated, may hold values from 0.1 to 1.9
- norm_shift_end: float32 [128], replicated, may hold values from -3 to 3
- proj_end: bfloat16 [128, 512], replicated, may hold values from -16 to 16
- bias_weight_end: bfloat16 [128, 4], replicated, may hold values from -1 to 1
- gate_bias_end: float32 [128], replicated, may hold values from -4 to 4
- out_weight_end: bfloat16 [128, 128], replicated, may hold values from -0.5 to 0.5
- out_bias_end: float32 [128], replicated, may hold values from -3 to 3
Outputs:
- updated_pair: float32 [512, 512, 128], P(('rb', 'cb'))
The draws below stay inside these ranges and needn't reach their ends.
All inputs are finite; a program needn't handle non-finite values.
Results may differ from the reference program's by a relative error of at most 0.0065.
The reference program's roundings to bfloat16 on the way (of `normed`, `pair_bias`, `weights` and `gated`) count: a program that leaves them out, or rounds other values in their place, can miss the bound.
Values may be sent and summed in bfloat16 or wider, within the bound.
A program may use at most 64 MiB of HBM per device.

```python
import jax
import jax.numpy as jnp
from jax import lax

C = 128
H = 4
HEAD = 32
N = 512


def make_proj(key, spread, first_gain, second_gain):
    width = H * HEAD
    base = jax.random.normal(key, (C, 4 * width), jnp.float32) * spread
    columns = jnp.arange(4 * width)
    in_key = (columns >= width) & (columns < 2 * width)
    head_of = columns % width // HEAD
    source = jnp.roll(base, width, axis=1)
    factor = jnp.where(head_of == 0, first_gain, jnp.where(head_of == 1, second_gain, 0.0))
    strong = in_key & (factor > 0.0)
    return jnp.clip(jnp.where(strong, source * factor, base), -16.0, 16.0)


def draw_proj_start(key, part):
    key = jax.random.fold_in(key, 11)
    return make_proj(key, 1.0 / jnp.sqrt(jnp.float32(C)), 0.0, 0.0).astype(jnp.bfloat16)


def draw_proj_end(key, part):
    key = jax.random.fold_in(key, 23)
    return make_proj(key, 1.0 / jnp.sqrt(jnp.float32(C)), 0.0, 0.0).astype(jnp.bfloat16)


def level_of(stream_key, shape, cuts, low, high):
    loudness = 1.0
    for position, shards_of in cuts:
        steps = jax.random.uniform(jax.random.fold_in(jax.random.fold_in(stream_key, 6), position), (shards_of,), jnp.float32, low / len(cuts), high / len(cuts))
        loudness = loudness * jnp.repeat(jnp.exp(steps), shape[position] // shards_of).reshape((-1,) + (1,) * (len(shape) - 1 - position))
    return loudness


def bell_draw(rng, extent, deviation, reach, shards=(), dtype=jnp.bfloat16):
    drawn = jax.random.normal(rng, extent, jnp.float32) * deviation
    if len(shards) > 0:
        drawn = level_of(rng, extent, shards, -0.22, 0.18) * drawn
    return jnp.clip(drawn, min=-reach, max=reach).astype(dtype)


def setup_inputs(seed: int = 0) -> dict:
    seeds = jax.random.split(jax.random.key(seed), 16)
    pair_map = bell_draw(seeds[0], (N, N, C), 1.0, 6.0, ((0, 128),), jnp.float32)
    norm_gain_start = jnp.clip(1.0 + 0.18 * jax.random.normal(seeds[1], (C,), jnp.float32), 0.1, 1.9)
    norm_shift_start = bell_draw(seeds[2], (C,), 0.5, 3.0, (), jnp.float32)
    proj_start = draw_proj_start(jax.random.fold_in(seeds[15], 71), 0)
    bias_weight_start = bell_draw(seeds[4], (C, H), (C // 4) ** -0.5, 1.0)
    gate_bias_start = bell_draw(seeds[5], (H * HEAD,), 1.0, 4.0, (), jnp.float32)
    out_weight_start = bell_draw(seeds[6], (H * HEAD, C), (H * HEAD) ** -0.5, 0.5)
    out_bias_start = bell_draw(seeds[7], (C,), 0.5, 3.0, (), jnp.float32)
    norm_gain_end = jnp.clip(1.0 + 0.18 * jax.random.normal(seeds[8], (C,), jnp.float32), 0.1, 1.9)
    norm_shift_end = bell_draw(seeds[9], (C,), 0.5, 3.0, (), jnp.float32)
    proj_end = draw_proj_end(jax.random.fold_in(seeds[15], 71), 0)
    bias_weight_end = bell_draw(seeds[11], (C, H), (C // 4) ** -0.5, 1.0)
    gate_bias_end = bell_draw(seeds[12], (H * HEAD,), 1.0, 4.0, (), jnp.float32)
    out_weight_end = bell_draw(seeds[13], (H * HEAD, C), (H * HEAD) ** -0.5, 0.5)
    out_bias_end = bell_draw(seeds[14], (C,), 0.5, 3.0, (), jnp.float32)
    return {"pair_map": pair_map, "norm_gain_start": norm_gain_start, "norm_shift_start": norm_shift_start, "proj_start": proj_start, "bias_weight_start": bias_weight_start, "gate_bias_start": gate_bias_start, "out_weight_start": out_weight_start, "out_bias_start": out_bias_start, "norm_gain_end": norm_gain_end, "norm_shift_end": norm_shift_end, "proj_end": proj_end, "bias_weight_end": bias_weight_end, "gate_bias_end": gate_bias_end, "out_weight_end": out_weight_end, "out_bias_end": out_bias_end}


def attend(pair, gain, shift, proj, bias_weight, gate_bias, out_weight, out_bias):
    width = H * HEAD
    mean = lax.optimization_barrier(jnp.mean(pair, axis=-1, keepdims=True))
    varia = lax.optimization_barrier(jnp.mean((pair - mean) ** 2, axis=-1, keepdims=True))
    normed = ((pair - mean) / jnp.sqrt(varia + 1e-05) * gain + shift).astype(jnp.bfloat16)
    flat = normed.reshape(N * N, C)
    projected = jnp.dot(flat, proj, preferred_element_type=jnp.float32)
    query = (projected[:, :width] / jnp.sqrt(jnp.float32(HEAD))).astype(jnp.bfloat16).reshape(N, N, H, HEAD)
    keys = projected[:, width:2 * width].astype(jnp.bfloat16).reshape(N, N, H, HEAD)
    values = projected[:, 2 * width:3 * width].astype(jnp.bfloat16).reshape(N, N, H, HEAD)
    gate = jax.nn.sigmoid(projected[:, 3 * width:] + gate_bias).reshape(N, N, width)
    pair_bias = jnp.einsum('jkc,ch->jhk', normed.astype(jnp.float32), bias_weight.astype(jnp.float32)).astype(jnp.bfloat16)
    bias_wide = pair_bias.astype(jnp.float32)

    def one_row(args):
        row_q, row_k, row_v, row_g, row_z = args
        scores = jnp.einsum('jhc,khc->jhk', row_q.astype(jnp.float32), row_k.astype(jnp.float32)) + bias_wide
        weights = jax.nn.softmax(scores, axis=-1).astype(jnp.bfloat16)
        attended = jnp.einsum('jhk,khc->jhc', weights.astype(jnp.float32), row_v.astype(jnp.float32)).reshape(N, width)
        gated = (row_g * attended).astype(jnp.bfloat16)
        return row_z + jnp.dot(gated, out_weight, preferred_element_type=jnp.float32) + out_bias
    return lax.map(one_row, (query, keys, values, gate, pair))

def reference(pair_map, norm_gain_start, norm_shift_start, proj_start, bias_weight_start, gate_bias_start, out_weight_start, out_bias_start, norm_gain_end, norm_shift_end, proj_end, bias_weight_end, gate_bias_end, out_weight_end, out_bias_end):
    after_start = attend(pair_map, norm_gain_start, norm_shift_start, proj_start, bias_weight_start, gate_bias_start, out_weight_start, out_bias_start)
    flipped = jnp.transpose(after_start, (1, 0, 2))
    ended = attend(flipped, norm_gain_end, norm_shift_end, proj_end, bias_weight_end, gate_bias_end, out_weight_end, out_bias_end)
    return jnp.transpose(ended, (1, 0, 2))
```

```python
import functools

import jax
import jax.numpy as jnp
from jax import lax
from jax.experimental import pallas as pl
from jax.experimental.pallas import tpu as pltpu
from jax.sharding import PartitionSpec as P

H = 4
HEAD = 32
WIDTH = H * HEAD
ROWS = 4
N = 512
C = 128
DEV = 128
MESH = pl.DeviceIdType.MESH
f32 = jnp.float32
bf16 = jnp.bfloat16

ORDERS = (("x", "y", "z"), ("y", "z", "x"), ("z", "x", "y"), ("x", "z", "y"))


def where_am_i():
    rb, cb = lax.axis_index("rb"), lax.axis_index("cb")
    return {
        "z": rb // 4,
        "y": (cb % 2) * 2 + (rb // 2) % 2,
        "x": cb // 2,
        "core": rb % 2,
    }


def device_of(at):
    return (at["z"] * 4 + (at["y"] % 2) * 2 + at["core"], at["x"] * 2 + at["y"] // 2)


def slot_y(y):
    return (y % 2) * 2 + y // 2


def slot_of(at):
    return at["z"] * 32 + slot_y(at["y"]) * 8 + at["x"] * 2 + at["core"]


def shifted(at, axis, by):
    size = 2 if axis == "core" else 4
    return {**at, axis: (at[axis] + by) % size}


def perms():
    row = lax.broadcasted_iota(jnp.int32, (256, 256), 0)
    col = lax.broadcasted_iota(jnp.int32, (256, 256), 1)

    def slot(n):
        return (n % 2) * 8 + ((n // 2) % 4) * 2 + n // 8

    a, n, b = row // 64, (row // 4) % 16, row % 4
    to_rows = jnp.where(col == slot(n) * 16 + a * 4 + b, 1.0, 0.0).astype(bf16)
    a, n, b = col // 64, (col // 4) % 16, col % 4
    to_slots = jnp.where(row == slot(n) * 16 + b * 4 + a, 1.0, 0.0).astype(bf16)
    return to_rows, to_slots


def layer_norm(pair, gain, shift):
    mean = jnp.mean(pair, axis=-1, keepdims=True)
    away = pair - mean
    varia = jnp.mean(away * away, axis=-1, keepdims=True)
    return (away / jnp.sqrt(varia + 1e-05) * gain + shift).astype(bf16)


def bias_slab(normed_ref, bias_weight):
    pick = lax.broadcasted_iota(jnp.int32, (16, H), 0) // 4 == lax.broadcasted_iota(jnp.int32, (16, H), 1)
    wide = lax.dot_general(
        jnp.where(pick, 1.0, 0.0).astype(bf16), bias_weight, (((1,), (1,)), ((), ())), preferred_element_type=f32
    )
    row = lax.broadcasted_iota(jnp.int32, (16, C), 0) % 4
    total = jnp.zeros((16, N), f32)
    for j in range(ROWS):
        mine = jnp.where(row == j, wide, 0.0).astype(bf16)
        total += lax.dot_general(mine, normed_ref[j], (((1,), (1,)), ((), ())), preferred_element_type=f32)
    return total.astype(bf16)


def gather_copy(bias, at, chunk, phase, by, send_sem, recv_sem):
    z, y, x, core = at["z"], slot_y(at["y"]), at["x"], at["core"]
    lanes = pl.ds(chunk * 128, 128)
    done = ("x", "y", "z") if phase == 3 else ORDERS[chunk][:phase]
    axis = "core" if phase == 3 else ORDERS[chunk][phase]
    all4 = pl.ds(0, 4)
    part = bias.at[
        all4 if "z" in done else z,
        all4 if "y" in done else y,
        all4 if "x" in done else x,
        core,
        :,
        lanes,
    ]
    return pltpu.make_async_remote_copy(
        src_ref=part,
        dst_ref=part,
        send_sem=send_sem.at[chunk, phase, by - 1],
        recv_sem=recv_sem.at[chunk, phase, by - 1],
        device_id=device_of(shifted(at, axis, by)),
        device_id_type=MESH,
    )


def offsets(phase):
    return (1,) if phase == 3 else (1, 2, 3)


def gather_start(bias, at, phase, send_sem, recv_sem):
    for chunk in range(4):
        if phase > 0:
            for by in offsets(phase - 1):
                gather_copy(bias, at, chunk, phase - 1, by, send_sem, recv_sem).wait_recv()
        for by in offsets(phase):
            gather_copy(bias, at, chunk, phase, by, send_sem, recv_sem).start()


def gather_end(bias, at, send_sem, recv_sem):
    for chunk in range(4):
        gather_copy(bias, at, chunk, 3, 1, send_sem, recv_sem).wait_recv()


def gather_drain(bias, at, send_sem, recv_sem):
    for phase in range(4):
        for chunk in range(4):
            for by in offsets(phase):
                gather_copy(bias, at, chunk, phase, by, send_sem, recv_sem).wait_send()


def spread_bias(bias, wide, to_rows):
    for z in range(4):
        for y in range(2):
            slabs = bias[z, 2 * y : 2 * y + 2].reshape(256, N)
            rows = jnp.dot(to_rows, slabs, preferred_element_type=f32)
            first = (z * 2 + y) * 64
            for h in range(H):
                wide[h, first : first + 64, :] = rows[h * 64 : (h + 1) * 64]


def projections(normed_ref, proj, gate_bias, query, keys, values, gate):
    for i in range(ROWS):
        out = jnp.dot(normed_ref[i], proj, preferred_element_type=f32)
        query[i] = (out[:, :WIDTH] / jnp.sqrt(f32(HEAD))).astype(bf16)
        keys[i] = out[:, WIDTH : 2 * WIDTH].astype(bf16)
        values[i] = out[:, 2 * WIDTH : 3 * WIDTH].astype(bf16)
        gate[i] = jax.nn.sigmoid(out[:, 3 * WIDTH :] + gate_bias)


def head_lanes(h, shape):
    return lax.broadcasted_iota(jnp.int32, shape, len(shape) - 1) // HEAD == h


def attention_row(i, query, keys, values, gate, wide):
    q, k, v = query[i], keys[i], values[i]
    total = None
    for h in range(H):
        lanes = head_lanes(h, (N, C))
        q_h = jnp.where(lanes, q, 0.0).astype(bf16)
        scores = lax.dot_general(q_h, k, (((1,), (1,)), ((), ())), preferred_element_type=f32) + wide[h]
        top = jnp.max(scores, axis=-1, keepdims=True)
        weights = jnp.exp(scores - top).astype(bf16)
        v_h = jnp.concatenate(
            [jnp.where(lanes, v, 0.0).astype(bf16), jnp.where(lanes, 1.0, 0.0).astype(bf16)], axis=1
        )
        part = jnp.dot(weights, v_h, preferred_element_type=f32)
        total = part if total is None else total + part
    return (gate[i] * (total[:, :WIDTH] / total[:, WIDTH:])).astype(bf16)


def exchange(at, send, recv, send_sem, recv_sem):
    me = slot_of(at)
    recv[me] = send[me]

    def start(o, carry):
        to = {
            "z": (at["z"] + o // 32) % 4,
            "y": (at["y"] + (o // 8) % 4) % 4,
            "x": (at["x"] + (o // 2) % 4) % 4,
            "core": (at["core"] + o % 2) % 2,
        }
        pltpu.make_async_remote_copy(
            src_ref=send.at[slot_of(to)],
            dst_ref=recv.at[me],
            send_sem=send_sem,
            recv_sem=recv_sem,
            device_id=device_of(to),
            device_id_type=MESH,
        ).start()
        return carry

    lax.fori_loop(1, DEV, start, 0)
    others = pl.ds(0, DEV - 1)
    whole = pltpu.make_async_remote_copy(
        src_ref=send.at[others],
        dst_ref=recv.at[others],
        send_sem=send_sem,
        recv_sem=recv_sem,
        device_id=device_of(shifted(at, "core", 1)),
        device_id_type=MESH,
    )
    whole.wait_recv()
    whole.wait_send()


def to_send(rows, send, to_slots):
    for g in range(8):
        part = jnp.concatenate([rows[i, g * 64 : (g + 1) * 64, :] for i in range(ROWS)], axis=0)
        moved = jnp.dot(to_slots, part, preferred_element_type=f32).astype(bf16)
        send[g * 16 : (g + 1) * 16] = moved.reshape(16, 16, C)


def from_recv(recv, rows, to_rows):
    for g in range(8):
        part = recv[g * 16 : (g + 1) * 16].reshape(256, C)
        moved = jnp.dot(to_rows, part, preferred_element_type=f32).astype(bf16)
        for i in range(ROWS):
            rows[i, g * 64 : (g + 1) * 64, :] = moved[i * 64 : (i + 1) * 64]


def kernel(
    pair,
    gain_s, shift_s, proj_s, bias_weight_s, gate_bias_s, out_weight_s, out_bias_s,
    gain_e, shift_e, proj_e, bias_weight_e, gate_bias_e, out_weight_e, out_bias_e,
    out,
    normed, query, keys, values, gate, wide, rows,
    bias_s, bias_e, send_a, recv_a, send_b, recv_b,
    g_send_s, g_recv_s, g_send_e, g_recv_e, x_send, x_recv,
):
    at = where_am_i()
    barrier = pltpu.get_barrier_semaphore()
    greet = [shifted(at, axis, by) for axis in ("x", "y", "z") for by in (1, 2, 3)] + [shifted(at, "core", 1)]
    for other in greet:
        pl.semaphore_signal(barrier, inc=1, device_id=device_of(other), device_id_type=MESH)

    z, y, x, core = at["z"], slot_y(at["y"]), at["x"], at["core"]
    to_rows, to_slots = perms()
    vec = lambda ref: ref[...].reshape(1, C)

    def norm_row(i, carry):
        normed[i] = layer_norm(pair[i], vec(gain_s), vec(shift_s))
        return carry

    lax.fori_loop(0, ROWS, norm_row, 0)
    bias_s[z, y, x, core] = bias_slab(normed, bias_weight_s[...])
    pl.semaphore_wait(barrier, len(greet))
    gather_start(bias_s, at, 0, g_send_s, g_recv_s)
    projections(normed, proj_s[...], vec(gate_bias_s), query, keys, values, gate)
    for phase in (1, 2, 3):
        gather_start(bias_s, at, phase, g_send_s, g_recv_s)
    gather_end(bias_s, at, g_send_s, g_recv_s)
    spread_bias(bias_s, wide, to_rows)

    def start_row(i, carry):
        gated = attention_row(i, query, keys, values, gate, wide)
        update = jnp.dot(gated, out_weight_s[...], preferred_element_type=f32)
        after = pair[i] + update + vec(out_bias_s)
        out[i] = after
        rows[i] = layer_norm(after, vec(gain_e), vec(shift_e))
        return carry

    lax.fori_loop(0, ROWS, start_row, 0)
    to_send(rows, send_a, to_slots)
    exchange(at, send_a, recv_a, x_send.at[0], x_recv.at[0])
    from_recv(recv_a, normed, to_rows)

    bias_e[z, y, x, core] = bias_slab(normed, bias_weight_e[...])
    gather_start(bias_e, at, 0, g_send_e, g_recv_e)
    projections(normed, proj_e[...], vec(gate_bias_e), query, keys, values, gate)
    for phase in (1, 2, 3):
        gather_start(bias_e, at, phase, g_send_e, g_recv_e)
    gather_end(bias_e, at, g_send_e, g_recv_e)
    spread_bias(bias_e, wide, to_rows)

    def end_row(i, carry):
        rows[i] = attention_row(i, query, keys, values, gate, wide)
        return carry

    lax.fori_loop(0, ROWS, end_row, 0)
    to_send(rows, send_b, to_slots)
    exchange(at, send_b, recv_b, x_send.at[1], x_recv.at[1])
    from_recv(recv_b, rows, to_rows)

    def finish_row(i, carry):
        update = jnp.dot(rows[i], out_weight_e[...], preferred_element_type=f32)
        out[i] = out[i] + update + vec(out_bias_e)
        return carry

    lax.fori_loop(0, ROWS, finish_row, 0)
    gather_drain(bias_s, at, g_send_s, g_recv_s)
    gather_drain(bias_e, at, g_send_e, g_recv_e)


def body(*args):
    vmem = pl.BlockSpec(memory_space=pltpu.VMEM)
    slab = (4, 4, 4, 2, 16, N)
    return pl.pallas_call(
        kernel,
        out_shape=jax.ShapeDtypeStruct((ROWS, N, C), f32),
        in_specs=[vmem] * len(args),
        out_specs=vmem,
        scratch_shapes=[
            pltpu.VMEM((ROWS, N, C), bf16),
            pltpu.VMEM((ROWS, N, C), bf16),
            pltpu.VMEM((ROWS, N, C), bf16),
            pltpu.VMEM((ROWS, N, C), bf16),
            pltpu.VMEM((ROWS, N, C), f32),
            pltpu.VMEM((H, N, N), f32),
            pltpu.VMEM((ROWS, N, C), bf16),
            pltpu.VMEM(slab, bf16),
            pltpu.VMEM(slab, bf16),
            pltpu.VMEM((DEV, 16, C), bf16),
            pltpu.VMEM((DEV, 16, C), bf16),
            pltpu.VMEM((DEV, 16, C), bf16),
            pltpu.VMEM((DEV, 16, C), bf16),
            pltpu.SemaphoreType.DMA((4, 4, 3)),
            pltpu.SemaphoreType.DMA((4, 4, 3)),
            pltpu.SemaphoreType.DMA((4, 4, 3)),
            pltpu.SemaphoreType.DMA((4, 4, 3)),
            pltpu.SemaphoreType.DMA((2,)),
            pltpu.SemaphoreType.DMA((2,)),
        ],
        compiler_params=pltpu.CompilerParams(
            collective_id=0, has_side_effects=True, vmem_limit_bytes=56 << 20
        ),
    )(*args)


def solution(mesh):
    rows = P(("rb", "cb"), None, None)
    return jax.shard_map(body, mesh=mesh, in_specs=(rows,) + (P(),) * 14, out_specs=rows, check_vma=False)
```

```python
import functools

import jax
import jax.numpy as jnp
from jax import lax
from jax.experimental import pallas as pl
from jax.experimental.pallas import tpu as pltpu
from jax.sharding import PartitionSpec as P

H = 4
HEAD = 32
WIDTH = H * HEAD
ROWS = 4
N = 512
C = 128
DEV = 128
MESH = pl.DeviceIdType.MESH
f32 = jnp.float32
bf16 = jnp.bfloat16

LINES = ("z", "x", "y", "z")
STEPS = (2, 1, 3, 0)


def where_am_i():
    rb, cb = lax.axis_index("rb"), lax.axis_index("cb")
    return {
        "z": rb // 4,
        "y": (cb % 2) * 2 + (rb // 2) % 2,
        "x": cb // 2,
        "core": rb % 2,
    }


def device_of(at):
    return (at["z"] * 4 + (at["y"] % 2) * 2 + at["core"], at["x"] * 2 + at["y"] // 2)


def slot_y(y):
    return (y % 2) * 2 + y // 2


def slot_of(at):
    return at["z"] * 32 + slot_y(at["y"]) * 8 + at["x"] * 2 + at["core"]


def shifted(at, axis, by):
    size = 2 if axis == "core" else 4
    return {**at, axis: (at[axis] + by) % size}


def perms():
    row = lax.broadcasted_iota(jnp.int32, (256, 256), 0)
    col = lax.broadcasted_iota(jnp.int32, (256, 256), 1)

    def slot(n):
        return (n % 2) * 8 + ((n // 2) % 4) * 2 + n // 8

    a, n, b = row // 64, (row // 4) % 16, row % 4
    to_rows = jnp.where(col == slot(n) * 16 + a * 4 + b, 1.0, 0.0).astype(bf16)
    a, n, b = col // 64, (col // 4) % 16, col % 4
    to_slots = jnp.where(row == slot(n) * 16 + b * 4 + a, 1.0, 0.0).astype(bf16)
    return to_rows, to_slots


def lane_perm():
    row = lax.broadcasted_iota(jnp.int32, (512, 512), 0)
    col = lax.broadcasted_iota(jnp.int32, (512, 512), 1)
    a, n, b = col // 128, (col // 4) % 32, col % 4
    slot = n // 16 * 16 + (n % 2) * 8 + ((n // 2) % 4) * 2 + (n // 8) % 2
    return jnp.where(row == slot * 16 + a * 4 + b, 1.0, 0.0).astype(bf16)


def layer_norm(pair, gain, shift):
    mean = jnp.mean(pair, axis=-1, keepdims=True)
    away = pair - mean
    varia = jnp.mean(away * away, axis=-1, keepdims=True)
    return (away / jnp.sqrt(varia + 1e-05) * gain + shift).astype(bf16)


def bias_slab(normed, bias_rows):
    pick = lax.broadcasted_iota(jnp.int32, (16, H), 0) // 4 == lax.broadcasted_iota(jnp.int32, (16, H), 1)
    wide = jnp.dot(jnp.where(pick, 1.0, 0.0).astype(bf16), bias_rows, preferred_element_type=f32)
    row = lax.broadcasted_iota(jnp.int32, (16, C), 0) % 4
    total = None
    for i in range(ROWS):
        mine = jnp.where(row == i, wide, 0.0).astype(bf16)
        part = lax.dot_general(mine, normed[i], (((1,), (1,)), ((), ())), preferred_element_type=f32)
        total = part if total is None else total + part
    return total.astype(bf16)


def tiles(ref, count):
    return ref.at[pl.ds(0, count)]


def wait_for(ref, count, at, send_sem, recv_sem, sent):
    part = tiles(ref, count)
    copy = pltpu.make_async_remote_copy(
        src_ref=part,
        dst_ref=part,
        send_sem=send_sem,
        recv_sem=recv_sem,
        device_id=device_of(shifted(at, "core", 1)),
        device_id_type=MESH,
    )
    if sent:
        copy.wait_send()
    else:
        copy.wait_recv()


def part_of(bias, at, chunk, whole):
    all4 = pl.ds(0, 4)
    return bias.at[
        all4 if "z" in whole else at["z"],
        all4 if "y" in whole else slot_y(at["y"]),
        all4 if "x" in whole else at["x"],
        at["core"],
        :,
        pl.ds(chunk * 128, 128),
    ]


def push(part, to, send_sem, recv_sem):
    pltpu.make_async_remote_copy(
        src_ref=part,
        dst_ref=part,
        send_sem=send_sem,
        recv_sem=recv_sem,
        device_id=device_of(to),
        device_id_type=MESH,
    ).start()


def plane_of(chunk):
    return [axis for axis in ("z", "y", "x") if axis != LINES[chunk]]


def plane_peers(at, chunk):
    first, second = plane_of(chunk)
    for one in (2, 1, 3, 0):
        for two in (2, 1, 3, 0):
            if one or two:
                yield shifted(shifted(at, first, one), second, two)


def gather_plane(bias, at, chunk, send_sem, recv_sem):
    part = part_of(bias, at, chunk, ())
    for to in plane_peers(at, chunk):
        push(part, to, send_sem.at[chunk, 0], recv_sem.at[chunk, 0])


def gather_line(bias, at, chunk, send_sem, recv_sem, spare):
    wait_for(spare, 15, at, send_sem.at[chunk, 0], recv_sem.at[chunk, 0], False)
    part = part_of(bias, at, chunk, plane_of(chunk))
    for by in (2, 1, 3):
        push(part, shifted(at, LINES[chunk], by), send_sem.at[chunk, 1], recv_sem.at[chunk, 1])


def gather_core(bias, at, chunk, send_sem, recv_sem, spare):
    wait_for(spare, 48, at, send_sem.at[chunk, 1], recv_sem.at[chunk, 1], False)
    push(part_of(bias, at, chunk, ("z", "y", "x")), shifted(at, "core", 1), send_sem.at[chunk, 2], recv_sem.at[chunk, 2])


def gather_end(at, chunk, send_sem, recv_sem, spare):
    wait_for(spare, 64, at, send_sem.at[chunk, 2], recv_sem.at[chunk, 2], False)


def gather_drain(at, send_sem, recv_sem, spare):
    for chunk in range(4):
        for phase, count in ((0, 15), (1, 48), (2, 64)):
            wait_for(spare, count, at, send_sem.at[chunk, phase], recv_sem.at[chunk, phase], True)


def spread_start(bias, wide, to_rows):
    for z in range(4):
        for y in range(2):
            slabs = bias[z, 2 * y : 2 * y + 2].reshape(256, N)
            rows = jnp.dot(to_rows, slabs, preferred_element_type=f32)
            for h in range(H):
                first = h * 128 + y * 64
                wide[z, first : first + 64, :] = rows[h * 64 : (h + 1) * 64]


def spread_end(bias, wide, to_lanes):
    for z in range(4):
        for step in range(4):
            block = (z + STEPS[step]) % 4
            slabs = bias[z, :, :, :, :, step * 128 : (step + 1) * 128].reshape(512, 128)
            cols = lax.dot_general(slabs, to_lanes, (((0,), (0,)), ((), ())), preferred_element_type=f32)
            for h in range(H):
                wide[block, h * 128 : (h + 1) * 128, z * 128 : (z + 1) * 128] = cols[:, h * 128 : (h + 1) * 128]


def projections(normed_ref, proj, gate_bias, query, keys, values, gate):
    for i in range(ROWS):
        out = jnp.dot(normed_ref[i], proj, preferred_element_type=f32)
        query[i] = (out[:, :WIDTH] / jnp.sqrt(f32(HEAD))).astype(bf16)
        keys[i] = out[:, WIDTH : 2 * WIDTH].astype(bf16)
        values[i] = out[:, 2 * WIDTH : 3 * WIDTH].astype(bf16)
        gate[i] = jax.nn.sigmoid(out[:, 3 * WIDTH :] + gate_bias)


def head_lanes(h, shape):
    return lax.broadcasted_iota(jnp.int32, shape, len(shape) - 1) // HEAD == h


def attention_block(i, first, wide, query, keys, values, gate):
    here = pl.ds(first, 128)
    lanes = [head_lanes(h, (128, C)) for h in range(H)]
    q = query[i, here, :]
    q_heads = jnp.concatenate([jnp.where(lane, q, 0.0).astype(bf16) for lane in lanes], axis=0)
    scores = lax.dot_general(q_heads, keys[i], (((1,), (1,)), ((), ())), preferred_element_type=f32) + wide
    top = jnp.max(scores, axis=-1, keepdims=True)
    weights = jnp.exp(scores - top).astype(bf16)
    v_ones = jnp.concatenate([values[i], jnp.ones((N, C), bf16)], axis=1)
    sums = jnp.dot(weights, v_ones, preferred_element_type=f32)

    def own_head(cols):
        parts = [sums[h * 128 : (h + 1) * 128, cols : cols + WIDTH] for h in range(H)]
        return jnp.where(lanes[0], parts[0], jnp.where(lanes[1], parts[1], jnp.where(lanes[2], parts[2], parts[3])))

    return (gate[i, here, :] * (own_head(0) / own_head(WIDTH))).astype(bf16)


def send_block(at, step, block, blocks, send, recv, to_slots, send_sem, recv_sem):
    for g in range(2):
        part = jnp.concatenate([rows[g * 64 : (g + 1) * 64] for rows in blocks], axis=0)
        moved = jnp.dot(to_slots, part, preferred_element_type=f32).astype(bf16)
        send[pl.ds(block * 32 + g * 16, 16)] = moved.reshape(16, 16, C)
    me = slot_of(at)

    def start(o, carry):
        q = 31 - o
        to = {
            "z": block,
            "y": (at["y"] + q // 8) % 4,
            "x": (at["x"] + (q // 2) % 4) % 4,
            "core": (at["core"] + q % 2) % 2,
        }
        pltpu.make_async_remote_copy(
            src_ref=send.at[slot_of(to)],
            dst_ref=recv.at[me],
            send_sem=send_sem,
            recv_sem=recv_sem,
            device_id=device_of(to),
            device_id_type=MESH,
        ).start()
        return carry

    lax.fori_loop(0, 31, start, 0)

    @pl.when(step < 3)
    def _():
        start(31, 0)

    @pl.when(step == 3)
    def _():
        recv[me] = send[me]


def from_recv(recv, rows, to_rows):
    for g in range(8):
        part = recv[g * 16 : (g + 1) * 16].reshape(256, C)
        moved = jnp.dot(to_rows, part, preferred_element_type=f32).astype(bf16)
        for i in range(ROWS):
            rows[i, g * 64 : (g + 1) * 64, :] = moved[i * 64 : (i + 1) * 64]


def block_of(at, step):
    by = jnp.where(step == 0, STEPS[0], jnp.where(step == 1, STEPS[1], jnp.where(step == 2, STEPS[2], STEPS[3])))
    return (at["z"] + by) % 4


def kernel(
    pair,
    gain_s, shift_s, proj_s, bias_rows_s, gate_bias_s, out_weight_s, out_bias_s,
    gain_e, shift_e, proj_e, bias_rows_e, gate_bias_e, out_weight_e, out_bias_e,
    out,
    normed, query, keys, values, gate, wide, to_lanes,
    bias_s, bias_e, send_a, recv_a, send_b, recv_b,
    g_send_s, g_recv_s, g_send_e, g_recv_e, x_send, x_recv,
):
    at = where_am_i()
    barrier = pltpu.get_barrier_semaphore()
    greet = [shifted(at, axis, by) for axis in ("x", "y", "z") for by in (1, 2, 3)] + [shifted(at, "core", 1)]
    for one, two in (("x", "y"), ("x", "z"), ("y", "z")):
        greet += [shifted(shifted(at, one, i), two, j) for i in (1, 2, 3) for j in (1, 2, 3)]
    for other in greet:
        pl.semaphore_signal(barrier, inc=1, device_id=device_of(other), device_id_type=MESH)

    z, y, x, core = at["z"], slot_y(at["y"]), at["x"], at["core"]
    vec = lambda ref: ref[...].reshape(1, C)

    def norm_row(i, carry):
        normed[i] = layer_norm(pair[i], vec(gain_s), vec(shift_s))
        return carry

    lax.fori_loop(0, ROWS, norm_row, 0)
    bias_s[z, y, x, core] = bias_slab(normed, bias_rows_s[...])
    pl.semaphore_wait(barrier, len(greet))
    for chunk in range(4):
        gather_plane(bias_s, at, chunk, g_send_s, g_recv_s)
    projections(normed, proj_s[...], vec(gate_bias_s), query, keys, values, gate)
    to_rows, to_slots = perms()
    to_lanes[...] = lane_perm()
    for chunk in range(4):
        gather_line(bias_s, at, chunk, g_send_s, g_recv_s, recv_a)
    for chunk in range(4):
        gather_core(bias_s, at, chunk, g_send_s, g_recv_s, recv_a)
    for chunk in range(4):
        gather_end(at, chunk, g_send_s, g_recv_s, recv_a)
    spread_start(bias_s, wide, to_rows)

    def start_step(step, carry):
        block = block_of(at, step)
        first = pl.multiple_of(block * 128, 128)
        blocks = []
        for i in range(ROWS):
            gated = attention_block(i, first, wide[block], query, keys, values, gate)
            update = jnp.dot(gated, out_weight_s[...], preferred_element_type=f32)
            after = pair[i, pl.ds(first, 128), :] + update + vec(out_bias_s)
            out[i, pl.ds(first, 128), :] = after
            blocks.append(layer_norm(after, vec(gain_e), vec(shift_e)))
        slab = bias_slab(blocks, bias_rows_e[...])
        for s in range(4):

            @pl.when(step == s)
            def _(s=s):
                bias_e[z, y, x, core, :, s * 128 : (s + 1) * 128] = slab
                gather_plane(bias_e, at, s, g_send_e, g_recv_e)
                if s >= 2:
                    gather_line(bias_e, at, s - 2, g_send_e, g_recv_e, recv_b)

        send_block(at, step, block, blocks, send_a, recv_a, to_slots, x_send.at[0], x_recv.at[0])
        return carry

    lax.fori_loop(0, 4, start_step, 0)
    for chunk in (2, 3):
        gather_line(bias_e, at, chunk, g_send_e, g_recv_e, recv_b)
    for chunk in (0, 1):
        gather_core(bias_e, at, chunk, g_send_e, g_recv_e, recv_b)
    wait_for(recv_a, DEV - 1, at, x_send.at[0], x_recv.at[0], False)
    from_recv(recv_a, normed, to_rows)
    projections(normed, proj_e[...], vec(gate_bias_e), query, keys, values, gate)
    for chunk in (2, 3):
        gather_core(bias_e, at, chunk, g_send_e, g_recv_e, recv_b)
    for chunk in range(4):
        gather_end(at, chunk, g_send_e, g_recv_e, recv_b)
    spread_end(bias_e, wide, to_lanes[...])

    def end_step(step, carry):
        block = block_of(at, step)
        first = pl.multiple_of(block * 128, 128)
        blocks = [attention_block(i, first, wide[block], query, keys, values, gate) for i in range(ROWS)]
        send_block(at, step, block, blocks, send_b, recv_b, to_slots, x_send.at[1], x_recv.at[1])
        return carry

    lax.fori_loop(0, 4, end_step, 0)
    gather_drain(at, g_send_s, g_recv_s, recv_a)
    gather_drain(at, g_send_e, g_recv_e, recv_a)
    wait_for(recv_b, DEV - 1, at, x_send.at[1], x_recv.at[1], False)
    from_recv(recv_b, normed, to_rows)

    def finish_row(i, carry):
        update = jnp.dot(normed[i], out_weight_e[...], preferred_element_type=f32)
        out[i] = out[i] + update + vec(out_bias_e)
        return carry

    lax.fori_loop(0, ROWS, finish_row, 0)
    for trip in range(2):
        wait_for(recv_a, DEV - 1, at, x_send.at[trip], x_recv.at[trip], True)


def body(*args):
    args = [arg.T if arg.shape == (C, H) else arg for arg in args]
    vmem = pl.BlockSpec(memory_space=pltpu.VMEM)
    slab = (4, 4, 4, 2, 16, N)
    return pl.pallas_call(
        kernel,
        out_shape=jax.ShapeDtypeStruct((ROWS, N, C), f32),
        in_specs=[vmem] * len(args),
        out_specs=vmem,
        scratch_shapes=[
            pltpu.VMEM((ROWS, N, C), bf16),
            pltpu.VMEM((ROWS, N, C), bf16),
            pltpu.VMEM((ROWS, N, C), bf16),
            pltpu.VMEM((ROWS, N, C), bf16),
            pltpu.VMEM((ROWS, N, C), f32),
            pltpu.VMEM((4, H * 128, N), f32),
            pltpu.VMEM((512, 512), bf16),
            pltpu.VMEM(slab, bf16),
            pltpu.VMEM(slab, bf16),
            pltpu.VMEM((DEV, 16, C), bf16),
            pltpu.VMEM((DEV, 16, C), bf16),
            pltpu.VMEM((DEV, 16, C), bf16),
            pltpu.VMEM((DEV, 16, C), bf16),
            pltpu.SemaphoreType.DMA((4, 3)),
            pltpu.SemaphoreType.DMA((4, 3)),
            pltpu.SemaphoreType.DMA((4, 3)),
            pltpu.SemaphoreType.DMA((4, 3)),
            pltpu.SemaphoreType.DMA((2,)),
            pltpu.SemaphoreType.DMA((2,)),
        ],
        compiler_params=pltpu.CompilerParams(
            collective_id=0, has_side_effects=True, vmem_limit_bytes=56 << 20
        ),
    )(*args)


def solution(mesh):
    rows = P(("rb", "cb"), None, None)
    return jax.shard_map(body, mesh=mesh, in_specs=(rows,) + (P(),) * 14, out_specs=rows, check_vma=False)
```

```python
import functools

import jax
import jax.numpy as jnp
from jax import lax
from jax.experimental import pallas as pl
from jax.experimental.pallas import tpu as pltpu
from jax.sharding import PartitionSpec as P

H = 4
HEAD = 32
WIDTH = H * HEAD
ROWS = 4
N = 512
C = 128
DEV = 128
MESH = pl.DeviceIdType.MESH
f32 = jnp.float32
bf16 = jnp.bfloat16

LINES = ("z", "x", "y", "z")
STEPS = (2, 1, 3, 0)


def where_am_i():
    rb, cb = lax.axis_index("rb"), lax.axis_index("cb")
    return {
        "z": rb // 4,
        "y": (cb % 2) * 2 + (rb // 2) % 2,
        "x": cb // 2,
        "core": rb % 2,
    }


def device_of(at):
    return (at["z"] * 4 + (at["y"] % 2) * 2 + at["core"], at["x"] * 2 + at["y"] // 2)


def slot_y(y):
    return (y % 2) * 2 + y // 2


def slot_of(at):
    return at["z"] * 32 + slot_y(at["y"]) * 8 + at["x"] * 2 + at["core"]


def shifted(at, axis, by):
    size = 2 if axis == "core" else 4
    return {**at, axis: (at[axis] + by) % size}


def perms():
    row = lax.broadcasted_iota(jnp.int32, (256, 256), 0)
    col = lax.broadcasted_iota(jnp.int32, (256, 256), 1)

    def slot(n):
        return (n % 2) * 8 + ((n // 2) % 4) * 2 + n // 8

    a, n, b = row // 64, (row // 4) % 16, row % 4
    to_rows = jnp.where(col == slot(n) * 16 + a * 4 + b, 1.0, 0.0).astype(bf16)
    a, n, b = col // 64, (col // 4) % 16, col % 4
    to_slots = jnp.where(row == slot(n) * 16 + b * 4 + a, 1.0, 0.0).astype(bf16)
    return to_rows, to_slots


def lane_perm():
    row = lax.broadcasted_iota(jnp.int32, (512, 512), 0)
    col = lax.broadcasted_iota(jnp.int32, (512, 512), 1)
    a, n, b = col // 128, (col // 4) % 32, col % 4
    slot = n // 16 * 16 + (n % 2) * 8 + ((n // 2) % 4) * 2 + (n // 8) % 2
    return jnp.where(row == slot * 16 + a * 4 + b, 1.0, 0.0).astype(bf16)


def layer_norm(pair, gain, shift):
    mean = jnp.mean(pair, axis=-1, keepdims=True)
    away = pair - mean
    varia = jnp.mean(away * away, axis=-1, keepdims=True)
    return (away / jnp.sqrt(varia + 1e-05) * gain + shift).astype(bf16)


def bias_slab(normed, bias_rows):
    pick = lax.broadcasted_iota(jnp.int32, (16, H), 0) // 4 == lax.broadcasted_iota(jnp.int32, (16, H), 1)
    wide = jnp.dot(jnp.where(pick, 1.0, 0.0).astype(bf16), bias_rows, preferred_element_type=f32)
    row = lax.broadcasted_iota(jnp.int32, (16, C), 0) % 4
    total = None
    for i in range(ROWS):
        mine = jnp.where(row == i, wide, 0.0).astype(bf16)
        part = lax.dot_general(mine, normed[i], (((1,), (1,)), ((), ())), preferred_element_type=f32)
        total = part if total is None else total + part
    return total.astype(bf16)


def tiles(ref, count):
    return ref.at[pl.ds(0, count)]


def wait_for(ref, count, at, send_sem, recv_sem, sent):
    part = tiles(ref, count)
    copy = pltpu.make_async_remote_copy(
        src_ref=part,
        dst_ref=part,
        send_sem=send_sem,
        recv_sem=recv_sem,
        device_id=device_of(shifted(at, "core", 1)),
        device_id_type=MESH,
    )
    if sent:
        copy.wait_send()
    else:
        copy.wait_recv()


def part_of(bias, at, chunk, whole):
    all4 = pl.ds(0, 4)
    return bias.at[
        all4 if "z" in whole else at["z"],
        all4 if "y" in whole else slot_y(at["y"]),
        all4 if "x" in whole else at["x"],
        at["core"],
        :,
        pl.ds(chunk * 128, 128),
    ]


def push(part, to, send_sem, recv_sem):
    pltpu.make_async_remote_copy(
        src_ref=part,
        dst_ref=part,
        send_sem=send_sem,
        recv_sem=recv_sem,
        device_id=device_of(to),
        device_id_type=MESH,
    ).start()


def plane_of(chunk):
    return [axis for axis in ("z", "y", "x") if axis != LINES[chunk]]


def plane_peers(at, chunk):
    first, second = plane_of(chunk)
    for one in (2, 1, 3, 0):
        for two in (2, 1, 3, 0):
            if one or two:
                yield shifted(shifted(at, first, one), second, two)


def gather_plane(bias, at, chunk, send_sem, recv_sem):
    part = part_of(bias, at, chunk, ())
    for to in plane_peers(at, chunk):
        push(part, to, send_sem.at[chunk, 0], recv_sem.at[chunk, 0])


def gather_line(bias, at, chunk, send_sem, recv_sem, spare):
    wait_for(spare, 15, at, send_sem.at[chunk, 0], recv_sem.at[chunk, 0], False)
    part = part_of(bias, at, chunk, plane_of(chunk))
    for by in (2, 1, 3):
        push(part, shifted(at, LINES[chunk], by), send_sem.at[chunk, 1], recv_sem.at[chunk, 1])


def gather_core(bias, at, chunk, send_sem, recv_sem, spare):
    wait_for(spare, 48, at, send_sem.at[chunk, 1], recv_sem.at[chunk, 1], False)
    push(part_of(bias, at, chunk, ("z", "y", "x")), shifted(at, "core", 1), send_sem.at[chunk, 2], recv_sem.at[chunk, 2])


def gather_end(at, chunk, send_sem, recv_sem, spare):
    wait_for(spare, 64, at, send_sem.at[chunk, 2], recv_sem.at[chunk, 2], False)


def gather_drain(at, send_sem, recv_sem, spare):
    for chunk in range(4):
        for phase, count in ((0, 15), (1, 48), (2, 64)):
            wait_for(spare, count, at, send_sem.at[chunk, phase], recv_sem.at[chunk, phase], True)


def spread_start(bias, wide, to_rows, chunk):
    here = slice(chunk * 128, (chunk + 1) * 128)
    for z in range(4):
        for y in range(2):
            slabs = bias[z, 2 * y : 2 * y + 2, :, :, :, here].reshape(256, 128)
            rows = jnp.dot(to_rows, slabs, preferred_element_type=f32)
            for h in range(H):
                first = h * 128 + y * 64
                wide[z, first : first + 64, here] = rows[h * 64 : (h + 1) * 64]


def spread_end(bias, wide, to_lanes, step):
    for z in range(4):
        block = (z + STEPS[step]) % 4
        slabs = bias[z, :, :, :, :, step * 128 : (step + 1) * 128].reshape(512, 128)
        cols = lax.dot_general(slabs, to_lanes, (((0,), (0,)), ((), ())), preferred_element_type=f32)
        for h in range(H):
            wide[block, h * 128 : (h + 1) * 128, z * 128 : (z + 1) * 128] = cols[:, h * 128 : (h + 1) * 128]


def project(i, here, rows, proj, gate_bias, query, keys, values, gate):
    out = jnp.dot(rows, proj, preferred_element_type=f32)
    query[i, here, :] = (out[:, :WIDTH] / jnp.sqrt(f32(HEAD))).astype(bf16)
    keys[i, here, :] = out[:, WIDTH : 2 * WIDTH].astype(bf16)
    values[i, here, :] = out[:, 2 * WIDTH : 3 * WIDTH].astype(bf16)
    gate[i, here, :] = jax.nn.sigmoid(out[:, 3 * WIDTH :] + gate_bias)


def head_lanes(h, shape):
    return lax.broadcasted_iota(jnp.int32, shape, len(shape) - 1) // HEAD == h


def pre_scores(block, query, keys, raw):
    lanes = [head_lanes(h, (128, C)) for h in range(H)]
    for i in range(ROWS):
        q = query[i, pl.ds(pl.multiple_of(block * 128, 128), 128), :]
        q_heads = jnp.concatenate([jnp.where(lane, q, 0.0).astype(bf16) for lane in lanes], axis=0)
        raw[block, i] = lax.dot_general(q_heads, keys[i], (((1,), (1,)), ((), ())), preferred_element_type=f32)


def attention_block(i, block, raw, wide, values, gate):
    here = pl.ds(pl.multiple_of(block * 128, 128), 128)
    lanes = [head_lanes(h, (128, C)) for h in range(H)]
    scores = raw[block, i] + wide[block]
    top = jnp.max(scores, axis=-1, keepdims=True)
    weights = jnp.exp(scores - top).astype(bf16)
    v_ones = jnp.concatenate([values[i], jnp.ones((N, C), bf16)], axis=1)
    sums = jnp.dot(weights, v_ones, preferred_element_type=f32)

    def own_head(cols):
        parts = [sums[h * 128 : (h + 1) * 128, cols : cols + WIDTH] for h in range(H)]
        return jnp.where(lanes[0], parts[0], jnp.where(lanes[1], parts[1], jnp.where(lanes[2], parts[2], parts[3])))

    return (gate[i, here, :] * (own_head(0) / own_head(WIDTH))).astype(bf16)


def send_block(at, step, block, blocks, send, recv, to_slots, send_sem, recv_sem):
    for g in range(2):
        part = jnp.concatenate([rows[g * 64 : (g + 1) * 64] for rows in blocks], axis=0)
        moved = jnp.dot(to_slots, part, preferred_element_type=f32).astype(bf16)
        send[pl.ds(block * 32 + g * 16, 16)] = moved.reshape(16, 16, C)
    me = slot_of(at)

    def start(o, carry):
        q = 31 - o
        to = {
            "z": block,
            "y": (at["y"] + q // 8) % 4,
            "x": (at["x"] + (q // 2) % 4) % 4,
            "core": (at["core"] + q % 2) % 2,
        }
        pltpu.make_async_remote_copy(
            src_ref=send.at[slot_of(to)],
            dst_ref=recv.at[me],
            send_sem=send_sem,
            recv_sem=recv_sem,
            device_id=device_of(to),
            device_id_type=MESH,
        ).start()
        return carry

    lax.fori_loop(0, 31, start, 0)

    @pl.when(step < 3)
    def _():
        start(31, 0)

    @pl.when(step == 3)
    def _():
        recv[me] = send[me]


def from_recv(recv, plane, to_rows):
    halves = []
    for g in range(2):
        part = recv[pl.ds(plane * 32 + g * 16, 16)].reshape(256, C)
        halves.append(jnp.dot(to_rows, part, preferred_element_type=f32).astype(bf16))
    return [jnp.concatenate([half[i * 64 : (i + 1) * 64] for half in halves], axis=0) for i in range(ROWS)]


def block_of(at, step):
    by = jnp.where(step == 0, STEPS[0], jnp.where(step == 1, STEPS[1], jnp.where(step == 2, STEPS[2], STEPS[3])))
    return (at["z"] + by) % 4


def kernel(
    pair_hbm,
    gain_s, shift_s, proj_s, bias_rows_s, gate_bias_s, out_weight_s, out_bias_s,
    gain_e, shift_e, proj_e, bias_rows_e, gate_bias_e, out_weight_e, out_bias_e,
    out_hbm,
    pair, normed, query, keys, values, gate, wide, raw, to_lanes,
    bias_s, bias_e, send_a, recv_a, send_b, recv_b,
    g_send_s, g_recv_s, g_send_e, g_recv_e, x_send, x_recv, in_sem, out_sem,
):
    at = where_am_i()
    barrier = pltpu.get_barrier_semaphore()
    greet = [shifted(at, axis, by) for axis in ("x", "y", "z") for by in (1, 2, 3)] + [shifted(at, "core", 1)]
    for one, two in (("x", "y"), ("x", "z"), ("y", "z")):
        greet += [shifted(shifted(at, one, i), two, j) for i in (1, 2, 3) for j in (1, 2, 3)]
    for other in greet:
        pl.semaphore_signal(barrier, inc=1, device_id=device_of(other), device_id_type=MESH)

    z, y, x, core = at["z"], slot_y(at["y"]), at["x"], at["core"]
    vec = lambda ref: ref[...].reshape(1, C)
    loads = [pltpu.make_async_copy(pair_hbm.at[i], pair.at[i], in_sem.at[i]) for i in range(ROWS)]
    for load in loads:
        load.start()
    for i in range(ROWS):
        loads[i].wait()
        normed[i] = layer_norm(pair[i], vec(gain_s), vec(shift_s))
    bias_s[z, y, x, core] = bias_slab(normed, bias_rows_s[...])
    pl.semaphore_wait(barrier, len(greet))
    for chunk in range(4):
        gather_plane(bias_s, at, chunk, g_send_s, g_recv_s)
    for i in range(ROWS):
        project(i, slice(None), normed[i], proj_s[...], vec(gate_bias_s), query, keys, values, gate)
    for block in range(2):
        pre_scores(block, query, keys, raw)
    for chunk in range(4):
        gather_line(bias_s, at, chunk, g_send_s, g_recv_s, recv_a)
    for block in range(2, 4):
        pre_scores(block, query, keys, raw)
    to_rows, to_slots = perms()
    to_lanes[...] = lane_perm()
    for chunk in range(4):
        gather_core(bias_s, at, chunk, g_send_s, g_recv_s, recv_a)
    for chunk in range(4):
        gather_end(at, chunk, g_send_s, g_recv_s, recv_a)
        spread_start(bias_s, wide, to_rows, chunk)

    def start_step(step, carry):
        block = block_of(at, step)
        here = pl.ds(pl.multiple_of(block * 128, 128), 128)
        blocks = []
        for i in range(ROWS):
            gated = attention_block(i, block, raw, wide, values, gate)
            update = jnp.dot(gated, out_weight_s[...], preferred_element_type=f32)
            after = pair[i, here, :] + update + vec(out_bias_s)
            pair[i, here, :] = after
            blocks.append(layer_norm(after, vec(gain_e), vec(shift_e)))
        slab = bias_slab(blocks, bias_rows_e[...])
        for s in range(4):

            @pl.when(step == s)
            def _(s=s):
                bias_e[z, y, x, core, :, s * 128 : (s + 1) * 128] = slab
                gather_plane(bias_e, at, s, g_send_e, g_recv_e)
                if s >= 2:
                    gather_line(bias_e, at, s - 2, g_send_e, g_recv_e, recv_b)

        send_block(at, step, block, blocks, send_a, recv_a, to_slots, x_send.at[0, step], x_recv.at[0, step])
        return carry

    lax.fori_loop(0, 4, start_step, 0)

    def receive(step):
        plane = (z + 4 - STEPS[step]) % 4
        wait_for(recv_a, 32 if step < 3 else 31, at, x_send.at[0, step], x_recv.at[0, step], False)
        here = pl.ds(pl.multiple_of(plane * 128, 128), 128)
        for i, rows in enumerate(from_recv(recv_a, plane, to_rows)):
            project(i, here, rows, proj_e[...], vec(gate_bias_e), query, keys, values, gate)

    receive(0)
    receive(1)
    gather_line(bias_e, at, 2, g_send_e, g_recv_e, recv_b)
    receive(2)
    gather_line(bias_e, at, 3, g_send_e, g_recv_e, recv_b)
    for chunk in (0, 1):
        gather_core(bias_e, at, chunk, g_send_e, g_recv_e, recv_b)
    receive(3)
    for block in range(2):
        pre_scores(block, query, keys, raw)
    gather_core(bias_e, at, 2, g_send_e, g_recv_e, recv_b)
    for block in range(2, 4):
        pre_scores(block, query, keys, raw)
    gather_core(bias_e, at, 3, g_send_e, g_recv_e, recv_b)
    for chunk in range(4):
        gather_end(at, chunk, g_send_e, g_recv_e, recv_b)
        spread_end(bias_e, wide, to_lanes[...], chunk)

    def end_step(step, carry):
        block = block_of(at, step)
        blocks = [attention_block(i, block, raw, wide, values, gate) for i in range(ROWS)]
        send_block(at, step, block, blocks, send_b, recv_b, to_slots, x_send.at[1, step], x_recv.at[1, step])
        return carry

    lax.fori_loop(0, 4, end_step, 0)
    gather_drain(at, g_send_s, g_recv_s, recv_a)
    gather_drain(at, g_send_e, g_recv_e, recv_a)
    stores = []
    for step in range(4):
        plane = (z + 4 - STEPS[step]) % 4
        here = pl.ds(pl.multiple_of(plane * 128, 128), 128)
        wait_for(recv_b, 32 if step < 3 else 31, at, x_send.at[1, step], x_recv.at[1, step], False)
        for i, rows in enumerate(from_recv(recv_b, plane, to_rows)):
            update = jnp.dot(rows, out_weight_e[...], preferred_element_type=f32)
            pair[i, here, :] = pair[i, here, :] + update + vec(out_bias_e)
        stores.append(pltpu.make_async_copy(pair.at[:, here], out_hbm.at[:, here], out_sem.at[step]))
        stores[-1].start()
    for trip in range(2):
        for step in range(4):
            wait_for(recv_a, 32 if step < 3 else 31, at, x_send.at[trip, step], x_recv.at[trip, step], True)
    for store in stores:
        store.wait()


def body(*args):
    args = [arg.T if arg.shape == (C, H) else arg for arg in args]
    vmem = pl.BlockSpec(memory_space=pltpu.VMEM)
    slab = (4, 4, 4, 2, 16, N)
    return pl.pallas_call(
        kernel,
        out_shape=jax.ShapeDtypeStruct((ROWS, N, C), f32),
        in_specs=[pl.BlockSpec(memory_space=pl.ANY)] + [vmem] * (len(args) - 1),
        out_specs=pl.BlockSpec(memory_space=pl.ANY),
        scratch_shapes=[
            pltpu.VMEM((ROWS, N, C), f32),
            pltpu.VMEM((ROWS, N, C), bf16),
            pltpu.VMEM((ROWS, N, C), bf16),
            pltpu.VMEM((ROWS, N, C), bf16),
            pltpu.VMEM((ROWS, N, C), bf16),
            pltpu.VMEM((ROWS, N, C), f32),
            pltpu.VMEM((4, H * 128, N), f32),
            pltpu.VMEM((4, ROWS, H * 128, N), f32),
            pltpu.VMEM((512, 512), bf16),
            pltpu.VMEM(slab, bf16),
            pltpu.VMEM(slab, bf16),
            pltpu.VMEM((DEV, 16, C), bf16),
            pltpu.VMEM((DEV, 16, C), bf16),
            pltpu.VMEM((DEV, 16, C), bf16),
            pltpu.VMEM((DEV, 16, C), bf16),
            pltpu.SemaphoreType.DMA((4, 3)),
            pltpu.SemaphoreType.DMA((4, 3)),
            pltpu.SemaphoreType.DMA((4, 3)),
            pltpu.SemaphoreType.DMA((4, 3)),
            pltpu.SemaphoreType.DMA((2, 4)),
            pltpu.SemaphoreType.DMA((2, 4)),
            pltpu.SemaphoreType.DMA((4,)),
            pltpu.SemaphoreType.DMA((4,)),
        ],
        compiler_params=pltpu.CompilerParams(
            collective_id=0, has_side_effects=True, vmem_limit_bytes=56 << 20
        ),
    )(*args)


def solution(mesh):
    rows = P(("rb", "cb"), None, None)
    return jax.shard_map(body, mesh=mesh, in_specs=(rows,) + (P(),) * 14, out_specs=rows, check_vma=False)
```

```python
import functools

import jax
import jax.numpy as jnp
from jax import lax
from jax.experimental import pallas as pl
from jax.experimental.pallas import tpu as pltpu
from jax.sharding import PartitionSpec as P

H = 4
HEAD = 32
WIDTH = H * HEAD
ROWS = 4
N = 512
C = 128
DEV = 128
MESH = pl.DeviceIdType.MESH
f32 = jnp.float32
bf16 = jnp.bfloat16

LINES = (("z", "x", "y", "x"), ("z", "x", "y", "z"))
STEPS = (2, 1, 3, 0)


def where_am_i():
    rb, cb = lax.axis_index("rb"), lax.axis_index("cb")
    return {
        "z": rb // 4,
        "y": (cb % 2) * 2 + (rb // 2) % 2,
        "x": cb // 2,
        "core": rb % 2,
    }


def device_of(at):
    return (at["z"] * 4 + (at["y"] % 2) * 2 + at["core"], at["x"] * 2 + at["y"] // 2)


def slot_y(y):
    return (y % 2) * 2 + y // 2


def slot_of(at):
    return at["z"] * 32 + slot_y(at["y"]) * 8 + at["x"] * 2 + at["core"]


def shifted(at, axis, by):
    size = 2 if axis == "core" else 4
    return {**at, axis: (at[axis] + by) % size}


def perms():
    row = lax.broadcasted_iota(jnp.int32, (256, 256), 0)
    col = lax.broadcasted_iota(jnp.int32, (256, 256), 1)

    def slot(n):
        return (n % 2) * 8 + ((n // 2) % 4) * 2 + n // 8

    a, n, b = row // 64, (row // 4) % 16, row % 4
    to_rows = jnp.where(col == slot(n) * 16 + a * 4 + b, 1.0, 0.0).astype(bf16)
    a, n, b = col // 64, (col // 4) % 16, col % 4
    to_slots = jnp.where(row == slot(n) * 16 + b * 4 + a, 1.0, 0.0).astype(bf16)
    return to_rows, to_slots


def lane_perm():
    row = lax.broadcasted_iota(jnp.int32, (512, 512), 0)
    col = lax.broadcasted_iota(jnp.int32, (512, 512), 1)
    a, n, b = col // 128, (col // 4) % 32, col % 4
    slot = n // 16 * 16 + (n % 2) * 8 + ((n // 2) % 4) * 2 + (n // 8) % 2
    return jnp.where(row == slot * 16 + a * 4 + b, 1.0, 0.0).astype(bf16)


def layer_norm(pair, gain, shift):
    mean = jnp.mean(pair, axis=-1, keepdims=True)
    away = pair - mean
    varia = jnp.mean(away * away, axis=-1, keepdims=True)
    return (away / jnp.sqrt(varia + 1e-05) * gain + shift).astype(bf16)


def bias_slab(normed, bias_rows):
    pick = lax.broadcasted_iota(jnp.int32, (16, H), 0) // 4 == lax.broadcasted_iota(jnp.int32, (16, H), 1)
    wide = jnp.dot(jnp.where(pick, 1.0, 0.0).astype(bf16), bias_rows, preferred_element_type=f32)
    row = lax.broadcasted_iota(jnp.int32, (16, C), 0) % 4
    total = None
    for i in range(ROWS):
        mine = jnp.where(row == i, wide, 0.0).astype(bf16)
        part = lax.dot_general(mine, normed[i], (((1,), (1,)), ((), ())), preferred_element_type=f32)
        total = part if total is None else total + part
    return total.astype(bf16)


def tiles(ref, count):
    return ref.at[pl.ds(0, count)]


def wait_for(ref, count, at, send_sem, recv_sem, sent):
    part = tiles(ref, count)
    copy = pltpu.make_async_remote_copy(
        src_ref=part,
        dst_ref=part,
        send_sem=send_sem,
        recv_sem=recv_sem,
        device_id=device_of(shifted(at, "core", 1)),
        device_id_type=MESH,
    )
    if sent:
        copy.wait_send()
    else:
        copy.wait_recv()


def part_of(bias, at, chunk, whole):
    all4 = pl.ds(0, 4)
    return bias.at[
        all4 if "z" in whole else at["z"],
        all4 if "y" in whole else slot_y(at["y"]),
        all4 if "x" in whole else at["x"],
        at["core"],
        :,
        pl.ds(chunk * 128, 128),
    ]


def push(part, to, send_sem, recv_sem):
    pltpu.make_async_remote_copy(
        src_ref=part,
        dst_ref=part,
        send_sem=send_sem,
        recv_sem=recv_sem,
        device_id=device_of(to),
        device_id_type=MESH,
    ).start()


def along(at, chunk, act):
    lines = [core_lines[chunk] for core_lines in LINES]
    for core, line in enumerate(lines):
        if core == 1 and lines[0] == lines[1]:
            continue
        plane = [axis for axis in ("z", "y", "x") if axis != line]
        if lines[0] == lines[1]:
            act(line, plane)
        else:
            pl.when(at["core"] == core)(functools.partial(act, line, plane))


def gather_plane(bias, at, chunk, send_sem, recv_sem):
    part = part_of(bias, at, chunk, ())

    def act(line, plane):
        for one in (2, 1, 3, 0):
            for two in (2, 1, 3, 0):
                if one or two:
                    to = shifted(shifted(at, plane[0], one), plane[1], two)
                    push(part, to, send_sem.at[chunk, 0], recv_sem.at[chunk, 0])

    along(at, chunk, act)


def gather_line(bias, at, chunk, send_sem, recv_sem, spare):
    wait_for(spare, 15, at, send_sem.at[chunk, 0], recv_sem.at[chunk, 0], False)

    def act(line, plane):
        part = part_of(bias, at, chunk, plane)
        for by in (2, 1, 3):
            push(part, shifted(at, line, by), send_sem.at[chunk, by], recv_sem.at[chunk, by])
        push(part, shifted(at, "core", 1), send_sem.at[chunk, 4], recv_sem.at[chunk, 4])

    along(at, chunk, act)


def gather_core(bias, at, chunk, send_sem, recv_sem, spare):
    def act(line, plane):
        for by in (1, 3, 2):
            wait_for(spare, 16, at, send_sem.at[chunk, by], recv_sem.at[chunk, by], False)
            part = part_of(bias, shifted(at, line, 4 - by), chunk, plane)
            push(part, shifted(at, "core", 1), send_sem.at[chunk, 4], recv_sem.at[chunk, 4])

    along(at, chunk, act)


def gather_end(at, chunk, send_sem, recv_sem, spare):
    wait_for(spare, 64, at, send_sem.at[chunk, 4], recv_sem.at[chunk, 4], False)


def gather_drain(at, send_sem, recv_sem, spare):
    for chunk in range(4):
        for phase, count in ((0, 15), (1, 16), (2, 16), (3, 16), (4, 64)):
            wait_for(spare, count, at, send_sem.at[chunk, phase], recv_sem.at[chunk, phase], True)


def spread_start(bias, wide, to_rows, chunk):
    here = slice(chunk * 128, (chunk + 1) * 128)
    for z in range(4):
        for y in range(2):
            slabs = bias[z, 2 * y : 2 * y + 2, :, :, :, here].reshape(256, 128)
            rows = jnp.dot(to_rows, slabs, preferred_element_type=f32)
            for h in range(H):
                first = h * 128 + y * 64
                wide[z, first : first + 64, here] = rows[h * 64 : (h + 1) * 64]


def spread_end(bias, wide, to_lanes, step):
    for z in range(4):
        block = (z + STEPS[step]) % 4
        slabs = bias[z, :, :, :, :, step * 128 : (step + 1) * 128].reshape(512, 128)
        cols = lax.dot_general(slabs, to_lanes, (((0,), (0,)), ((), ())), preferred_element_type=f32)
        for h in range(H):
            wide[block, h * 128 : (h + 1) * 128, z * 128 : (z + 1) * 128] = cols[:, h * 128 : (h + 1) * 128]


def project(i, here, rows, proj, gate_bias, query, keys, values, gate):
    out = jnp.dot(rows, proj, preferred_element_type=f32)
    query[i, here, :] = (out[:, :WIDTH] / jnp.sqrt(f32(HEAD))).astype(bf16)
    keys[i, here, :] = out[:, WIDTH : 2 * WIDTH].astype(bf16)
    values[i, here, :] = out[:, 2 * WIDTH : 3 * WIDTH].astype(bf16)
    gate[i, here, :] = jax.nn.sigmoid(out[:, 3 * WIDTH :] + gate_bias)


def head_lanes(h, shape):
    return lax.broadcasted_iota(jnp.int32, shape, len(shape) - 1) // HEAD == h


def pre_scores(block, query, keys, raw):
    lanes = [head_lanes(h, (128, C)) for h in range(H)]
    for i in range(ROWS):
        q = query[i, pl.ds(pl.multiple_of(block * 128, 128), 128), :]
        q_heads = jnp.concatenate([jnp.where(lane, q, 0.0).astype(bf16) for lane in lanes], axis=0)
        raw[block, i] = lax.dot_general(q_heads, keys[i], (((1,), (1,)), ((), ())), preferred_element_type=f32)


def attention_block(i, block, raw, wide, values, gate):
    here = pl.ds(pl.multiple_of(block * 128, 128), 128)
    lanes = [head_lanes(h, (128, C)) for h in range(H)]
    scores = raw[block, i] + wide[block]
    top = jnp.max(scores, axis=-1, keepdims=True)
    weights = jnp.exp(scores - top).astype(bf16)
    v_ones = jnp.concatenate([values[i], jnp.ones((N, C), bf16)], axis=1)
    sums = jnp.dot(weights, v_ones, preferred_element_type=f32)

    def own_head(cols):
        parts = [sums[h * 128 : (h + 1) * 128, cols : cols + WIDTH] for h in range(H)]
        return jnp.where(lanes[0], parts[0], jnp.where(lanes[1], parts[1], jnp.where(lanes[2], parts[2], parts[3])))

    return (gate[i, here, :] * (own_head(0) / own_head(WIDTH))).astype(bf16)


def send_block(at, step, block, blocks, send, recv, to_slots, send_sem, recv_sem):
    for g in range(2):
        part = jnp.concatenate([rows[g * 64 : (g + 1) * 64] for rows in blocks], axis=0)
        moved = jnp.dot(to_slots, part, preferred_element_type=f32).astype(bf16)
        send[pl.ds(block * 32 + g * 16, 16)] = moved.reshape(16, 16, C)
    me = slot_of(at)

    ys = [(at["y"] + by) % 4 for by in range(4)]
    xs = [(at["x"] + by) % 4 for by in range(4)]
    cores = [at["core"], 1 - at["core"]]

    def start(q):
        to = {"z": block, "y": ys[q // 8], "x": xs[q // 2 % 4], "core": cores[q % 2]}
        pltpu.make_async_remote_copy(
            src_ref=send.at[slot_of(to)],
            dst_ref=recv.at[me],
            send_sem=send_sem,
            recv_sem=recv_sem,
            device_id=device_of(to),
            device_id_type=MESH,
        ).start()

    for q in range(31, 0, -1):
        start(q)

    @pl.when(step < 3)
    def _():
        start(0)

    @pl.when(step == 3)
    def _():
        recv[me] = send[me]


def from_recv(recv, plane, to_rows):
    halves = []
    for g in range(2):
        part = recv[pl.ds(plane * 32 + g * 16, 16)].reshape(256, C)
        halves.append(jnp.dot(to_rows, part, preferred_element_type=f32).astype(bf16))
    return [jnp.concatenate([half[i * 64 : (i + 1) * 64] for half in halves], axis=0) for i in range(ROWS)]


def block_of(at, step):
    by = jnp.where(step == 0, STEPS[0], jnp.where(step == 1, STEPS[1], jnp.where(step == 2, STEPS[2], STEPS[3])))
    return (at["z"] + by) % 4


def kernel(
    pair_hbm,
    gain_s, shift_s, proj_s, bias_rows_s, gate_bias_s, out_weight_s, out_bias_s,
    gain_e, shift_e, proj_e, bias_rows_e, gate_bias_e, out_weight_e, out_bias_e,
    out_hbm,
    pair, normed, query, keys, values, gate, wide, raw, to_lanes,
    bias_s, bias_e, send_a, recv_a, send_b, recv_b,
    g_send_s, g_recv_s, g_send_e, g_recv_e, x_send, x_recv, in_sem, out_sem,
):
    at = where_am_i()
    barrier = pltpu.get_barrier_semaphore()
    greet = [shifted(at, axis, by) for axis in ("x", "y", "z") for by in (1, 2, 3)] + [shifted(at, "core", 1)]
    for one, two in (("x", "y"), ("x", "z"), ("y", "z")):
        greet += [shifted(shifted(at, one, i), two, j) for i in (1, 2, 3) for j in (1, 2, 3)]
    for other in greet:
        pl.semaphore_signal(barrier, inc=1, device_id=device_of(other), device_id_type=MESH)

    z, y, x, core = at["z"], slot_y(at["y"]), at["x"], at["core"]
    vec = lambda ref: ref[...].reshape(1, C)
    loads = [pltpu.make_async_copy(pair_hbm.at[i], pair.at[i], in_sem.at[i]) for i in range(ROWS)]
    for load in loads:
        load.start()
    for i in range(ROWS):
        loads[i].wait()
        normed[i] = layer_norm(pair[i], vec(gain_s), vec(shift_s))
    bias_s[z, y, x, core] = bias_slab(normed, bias_rows_s[...])
    pl.semaphore_wait(barrier, len(greet))
    for chunk in range(4):
        gather_plane(bias_s, at, chunk, g_send_s, g_recv_s)
    for i in range(ROWS):
        project(i, slice(None), normed[i], proj_s[...], vec(gate_bias_s), query, keys, values, gate)
    for block in range(2):
        pre_scores(block, query, keys, raw)
    for chunk in range(4):
        gather_line(bias_s, at, chunk, g_send_s, g_recv_s, recv_a)
    for block in range(2, 4):
        pre_scores(block, query, keys, raw)
    to_rows, to_slots = perms()
    to_lanes[...] = lane_perm()
    for chunk in range(4):
        gather_core(bias_s, at, chunk, g_send_s, g_recv_s, recv_a)
    for chunk in range(4):
        gather_end(at, chunk, g_send_s, g_recv_s, recv_a)
        spread_start(bias_s, wide, to_rows, chunk)

    def start_step(step, carry):
        block = block_of(at, step)
        here = pl.ds(pl.multiple_of(block * 128, 128), 128)
        blocks = []
        for i in range(ROWS):
            gated = attention_block(i, block, raw, wide, values, gate)
            update = jnp.dot(gated, out_weight_s[...], preferred_element_type=f32)
            after = pair[i, here, :] + update + vec(out_bias_s)
            pair[i, here, :] = after
            blocks.append(layer_norm(after, vec(gain_e), vec(shift_e)))
        slab = bias_slab(blocks, bias_rows_e[...])
        for s in range(4):

            @pl.when(step == s)
            def _(s=s):
                bias_e[z, y, x, core, :, s * 128 : (s + 1) * 128] = slab
                gather_plane(bias_e, at, s, g_send_e, g_recv_e)
                if s >= 2:
                    gather_line(bias_e, at, s - 2, g_send_e, g_recv_e, recv_b)

        send_block(at, step, block, blocks, send_a, recv_a, to_slots, x_send.at[0, step], x_recv.at[0, step])
        return carry

    lax.fori_loop(0, 4, start_step, 0)

    def receive(step):
        plane = (z + 4 - STEPS[step]) % 4
        wait_for(recv_a, 32 if step < 3 else 31, at, x_send.at[0, step], x_recv.at[0, step], False)
        here = pl.ds(pl.multiple_of(plane * 128, 128), 128)
        for i, rows in enumerate(from_recv(recv_a, plane, to_rows)):
            project(i, here, rows, proj_e[...], vec(gate_bias_e), query, keys, values, gate)

    def settle(chunk):
        gather_end(at, chunk, g_send_e, g_recv_e, recv_b)
        spread_end(bias_e, wide, to_lanes[...], chunk)

    receive(0)
    receive(1)
    gather_line(bias_e, at, 2, g_send_e, g_recv_e, recv_b)
    receive(2)
    gather_line(bias_e, at, 3, g_send_e, g_recv_e, recv_b)
    for chunk in (0, 1):
        gather_core(bias_e, at, chunk, g_send_e, g_recv_e, recv_b)
    receive(3)
    for block in range(2):
        pre_scores(block, query, keys, raw)
    gather_core(bias_e, at, 2, g_send_e, g_recv_e, recv_b)
    settle(0)
    settle(1)
    for block in range(2, 4):
        pre_scores(block, query, keys, raw)
    gather_core(bias_e, at, 3, g_send_e, g_recv_e, recv_b)
    settle(2)
    settle(3)

    def end_step(step, carry):
        block = block_of(at, step)
        blocks = [attention_block(i, block, raw, wide, values, gate) for i in range(ROWS)]
        send_block(at, step, block, blocks, send_b, recv_b, to_slots, x_send.at[1, step], x_recv.at[1, step])
        return carry

    lax.fori_loop(0, 4, end_step, 0)
    gather_drain(at, g_send_s, g_recv_s, recv_a)
    gather_drain(at, g_send_e, g_recv_e, recv_a)
    stores = []
    for step in range(4):
        plane = (z + 4 - STEPS[step]) % 4
        here = pl.ds(pl.multiple_of(plane * 128, 128), 128)
        wait_for(recv_b, 32 if step < 3 else 31, at, x_send.at[1, step], x_recv.at[1, step], False)
        for i, rows in enumerate(from_recv(recv_b, plane, to_rows)):
            update = jnp.dot(rows, out_weight_e[...], preferred_element_type=f32)
            pair[i, here, :] = pair[i, here, :] + update + vec(out_bias_e)
        stores.append(pltpu.make_async_copy(pair.at[:, here], out_hbm.at[:, here], out_sem.at[step]))
        stores[-1].start()
    for trip in range(2):
        for step in range(4):
            wait_for(recv_a, 32 if step < 3 else 31, at, x_send.at[trip, step], x_recv.at[trip, step], True)
    for store in stores:
        store.wait()


def body(*args):
    args = [arg.T if arg.shape == (C, H) else arg for arg in args]
    vmem = pl.BlockSpec(memory_space=pltpu.VMEM)
    slab = (4, 4, 4, 2, 16, N)
    return pl.pallas_call(
        kernel,
        out_shape=jax.ShapeDtypeStruct((ROWS, N, C), f32),
        in_specs=[pl.BlockSpec(memory_space=pl.ANY)] + [vmem] * (len(args) - 1),
        out_specs=pl.BlockSpec(memory_space=pl.ANY),
        scratch_shapes=[
            pltpu.VMEM((ROWS, N, C), f32),
            pltpu.VMEM((ROWS, N, C), bf16),
            pltpu.VMEM((ROWS, N, C), bf16),
            pltpu.VMEM((ROWS, N, C), bf16),
            pltpu.VMEM((ROWS, N, C), bf16),
            pltpu.VMEM((ROWS, N, C), f32),
            pltpu.VMEM((4, H * 128, N), f32),
            pltpu.VMEM((4, ROWS, H * 128, N), f32),
            pltpu.VMEM((512, 512), bf16),
            pltpu.VMEM(slab, bf16),
            pltpu.VMEM(slab, bf16),
            pltpu.VMEM((DEV, 16, C), bf16),
            pltpu.VMEM((DEV, 16, C), bf16),
            pltpu.VMEM((DEV, 16, C), bf16),
            pltpu.VMEM((DEV, 16, C), bf16),
            pltpu.SemaphoreType.DMA((4, 5)),
            pltpu.SemaphoreType.DMA((4, 5)),
            pltpu.SemaphoreType.DMA((4, 5)),
            pltpu.SemaphoreType.DMA((4, 5)),
            pltpu.SemaphoreType.DMA((2, 4)),
            pltpu.SemaphoreType.DMA((2, 4)),
            pltpu.SemaphoreType.DMA((4,)),
            pltpu.SemaphoreType.DMA((4,)),
        ],
        compiler_params=pltpu.CompilerParams(
            collective_id=0, has_side_effects=True, vmem_limit_bytes=56 << 20
        ),
    )(*args)


def solution(mesh):
    rows = P(("rb", "cb"), None, None)
    return jax.shard_map(body, mesh=mesh, in_specs=(rows,) + (P(),) * 14, out_specs=rows, check_vma=False)
```

```python
import functools

import jax
import jax.numpy as jnp
from jax import lax
from jax.experimental import pallas as pl
from jax.experimental.pallas import tpu as pltpu
from jax.sharding import PartitionSpec as P

H = 4
HEAD = 32
WIDTH = H * HEAD
ROWS = 4
N = 512
C = 128
DEV = 128
MESH = pl.DeviceIdType.MESH
f32 = jnp.float32
bf16 = jnp.bfloat16

LINES = (("z", "x", "y", "x"), ("z", "x", "y", "z"))
STEPS = (2, 1, 3, 0)


def where_am_i():
    rb, cb = lax.axis_index("rb"), lax.axis_index("cb")
    return {
        "z": rb // 4,
        "y": (cb % 2) * 2 + (rb // 2) % 2,
        "x": cb // 2,
        "core": rb % 2,
    }


def device_of(at):
    return (at["z"] * 4 + (at["y"] % 2) * 2 + at["core"], at["x"] * 2 + at["y"] // 2)


def slot_y(y):
    return (y % 2) * 2 + y // 2


def slot_of(at):
    return at["z"] * 32 + slot_y(at["y"]) * 8 + at["x"] * 2 + at["core"]


def shifted(at, axis, by):
    size = 2 if axis == "core" else 4
    return {**at, axis: (at[axis] + by) % size}


def perms():
    row = lax.broadcasted_iota(jnp.int32, (256, 256), 0)
    col = lax.broadcasted_iota(jnp.int32, (256, 256), 1)

    def slot(n):
        return (n % 2) * 8 + ((n // 2) % 4) * 2 + n // 8

    a, n, b = row // 64, (row // 4) % 16, row % 4
    to_rows = jnp.where(col == slot(n) * 16 + a * 4 + b, 1.0, 0.0).astype(bf16)
    a, n, b = col // 64, (col // 4) % 16, col % 4
    to_slots = jnp.where(row == slot(n) * 16 + b * 4 + a, 1.0, 0.0).astype(bf16)
    return to_rows, to_slots


def lane_perm():
    row = lax.broadcasted_iota(jnp.int32, (512, 512), 0)
    col = lax.broadcasted_iota(jnp.int32, (512, 512), 1)
    a, n, b = col // 128, (col // 4) % 32, col % 4
    slot = n // 16 * 16 + (n % 2) * 8 + ((n // 2) % 4) * 2 + (n // 8) % 2
    return jnp.where(row == slot * 16 + a * 4 + b, 1.0, 0.0).astype(bf16)


def layer_norm(pair, gain, shift):
    mean = jnp.mean(pair, axis=-1, keepdims=True)
    away = pair - mean
    varia = jnp.mean(away * away, axis=-1, keepdims=True)
    return (away / jnp.sqrt(varia + 1e-05) * gain + shift).astype(bf16)


def bias_slab(normed, bias_rows):
    pick = lax.broadcasted_iota(jnp.int32, (16, H), 0) // 4 == lax.broadcasted_iota(jnp.int32, (16, H), 1)
    wide = jnp.dot(jnp.where(pick, 1.0, 0.0).astype(bf16), bias_rows, preferred_element_type=f32)
    row = lax.broadcasted_iota(jnp.int32, (16, C), 0) % 4
    total = None
    for i in range(ROWS):
        mine = jnp.where(row == i, wide, 0.0).astype(bf16)
        part = lax.dot_general(mine, normed[i], (((1,), (1,)), ((), ())), preferred_element_type=f32)
        total = part if total is None else total + part
    return total.astype(bf16)


def tiles(ref, count):
    return ref.at[pl.ds(0, count)]


def wait_for(ref, count, at, send_sem, recv_sem, sent):
    part = tiles(ref, count)
    copy = pltpu.make_async_remote_copy(
        src_ref=part,
        dst_ref=part,
        send_sem=send_sem,
        recv_sem=recv_sem,
        device_id=device_of(shifted(at, "core", 1)),
        device_id_type=MESH,
    )
    if sent:
        copy.wait_send()
    else:
        copy.wait_recv()


def part_of(bias, at, chunk, whole):
    all4 = pl.ds(0, 4)
    return bias.at[
        all4 if "z" in whole else at["z"],
        all4 if "y" in whole else slot_y(at["y"]),
        all4 if "x" in whole else at["x"],
        at["core"],
        :,
        pl.ds(chunk * 128, 128),
    ]


def push(part, to, send_sem, recv_sem):
    pltpu.make_async_remote_copy(
        src_ref=part,
        dst_ref=part,
        send_sem=send_sem,
        recv_sem=recv_sem,
        device_id=device_of(to),
        device_id_type=MESH,
    ).start()


def along(at, chunk, act):
    lines = [core_lines[chunk] for core_lines in LINES]
    for core, line in enumerate(lines):
        if core == 1 and lines[0] == lines[1]:
            continue
        plane = [axis for axis in ("z", "y", "x") if axis != line]
        if lines[0] == lines[1]:
            act(line, plane)
        else:
            pl.when(at["core"] == core)(functools.partial(act, line, plane))


def gather_plane(bias, at, chunk, send_sem, recv_sem):
    part = part_of(bias, at, chunk, ())

    def act(line, plane):
        for one in (2, 1, 3, 0):
            for two in (2, 1, 3, 0):
                if one or two:
                    to = shifted(shifted(at, plane[0], one), plane[1], two)
                    push(part, to, send_sem.at[chunk, one], recv_sem.at[chunk, one])

    along(at, chunk, act)


def gather_row(bias, at, chunk, one, send_sem, recv_sem, spare):
    wait_for(spare, 4 if one else 3, at, send_sem.at[chunk, one], recv_sem.at[chunk, one], False)

    def act(line, plane):
        part = part_of(bias, shifted(at, plane[0], 4 - one), chunk, plane[1:])
        for by in (2, 1, 3):
            push(part, shifted(at, line, by), send_sem.at[chunk, 4 + by], recv_sem.at[chunk, 4 + by])

    along(at, chunk, act)


def gather_line(bias, at, chunks, send_sem, recv_sem, spare):
    for one in (0, 1, 3, 2):
        for chunk in chunks:
            gather_row(bias, at, chunk, one, send_sem, recv_sem, spare)
    for chunk in chunks:
        along(
            at,
            chunk,
            lambda line, plane, chunk=chunk: push(
                part_of(bias, at, chunk, plane), shifted(at, "core", 1), send_sem.at[chunk, 4], recv_sem.at[chunk, 4]
            ),
        )


def gather_core(bias, at, chunk, send_sem, recv_sem, spare):
    def act(line, plane):
        for by in (1, 3, 2):
            wait_for(spare, 16, at, send_sem.at[chunk, 4 + by], recv_sem.at[chunk, 4 + by], False)
            part = part_of(bias, shifted(at, line, 4 - by), chunk, plane)
            push(part, shifted(at, "core", 1), send_sem.at[chunk, 4], recv_sem.at[chunk, 4])

    along(at, chunk, act)


def gather_end(at, chunk, send_sem, recv_sem, spare):
    wait_for(spare, 64, at, send_sem.at[chunk, 4], recv_sem.at[chunk, 4], False)


def gather_drain(at, send_sem, recv_sem, spare):
    for chunk in range(4):
        for phase, count in ((0, 3), (1, 4), (2, 4), (3, 4), (4, 64), (5, 16), (6, 16), (7, 16)):
            wait_for(spare, count, at, send_sem.at[chunk, phase], recv_sem.at[chunk, phase], True)


def spread_start(bias, wide, to_rows, chunk):
    here = slice(chunk * 128, (chunk + 1) * 128)
    for z in range(4):
        for y in range(2):
            slabs = bias[z, 2 * y : 2 * y + 2, :, :, :, here].reshape(256, 128)
            rows = jnp.dot(to_rows, slabs, preferred_element_type=f32)
            for h in range(H):
                first = h * 128 + y * 64
                wide[z, first : first + 64, here] = rows[h * 64 : (h + 1) * 64]


def spread_end(bias, wide, to_lanes, step):
    for z in range(4):
        block = (z + STEPS[step]) % 4
        slabs = bias[z, :, :, :, :, step * 128 : (step + 1) * 128].reshape(512, 128)
        cols = lax.dot_general(slabs, to_lanes, (((0,), (0,)), ((), ())), preferred_element_type=f32)
        for h in range(H):
            wide[block, h * 128 : (h + 1) * 128, z * 128 : (z + 1) * 128] = cols[:, h * 128 : (h + 1) * 128]


def project(i, here, rows, proj, gate_bias, query, keys, values, gate):
    out = jnp.dot(rows, proj, preferred_element_type=f32)
    query[i, here, :] = (out[:, :WIDTH] / jnp.sqrt(f32(HEAD))).astype(bf16)
    keys[i, here, :] = out[:, WIDTH : 2 * WIDTH].astype(bf16)
    values[i, here, :] = out[:, 2 * WIDTH : 3 * WIDTH].astype(bf16)
    gate[i, here, :] = jax.nn.sigmoid(out[:, 3 * WIDTH :] + gate_bias)


def head_lanes(h, shape):
    return lax.broadcasted_iota(jnp.int32, shape, len(shape) - 1) // HEAD == h


def pre_scores(block, query, keys, raw):
    lanes = [head_lanes(h, (128, C)) for h in range(H)]
    for i in range(ROWS):
        q = query[i, pl.ds(pl.multiple_of(block * 128, 128), 128), :]
        q_heads = jnp.concatenate([jnp.where(lane, q, 0.0).astype(bf16) for lane in lanes], axis=0)
        raw[block, i] = lax.dot_general(q_heads, keys[i], (((1,), (1,)), ((), ())), preferred_element_type=f32)


def attention_block(i, block, raw, wide, values, gate):
    here = pl.ds(pl.multiple_of(block * 128, 128), 128)
    lanes = [head_lanes(h, (128, C)) for h in range(H)]
    scores = raw[block, i] + wide[block]
    top = jnp.max(scores, axis=-1, keepdims=True)
    weights = jnp.exp(scores - top).astype(bf16)
    v_ones = jnp.concatenate([values[i], jnp.ones((N, C), bf16)], axis=1)
    sums = jnp.dot(weights, v_ones, preferred_element_type=f32)

    def own_head(cols):
        parts = [sums[h * 128 : (h + 1) * 128, cols : cols + WIDTH] for h in range(H)]
        return jnp.where(lanes[0], parts[0], jnp.where(lanes[1], parts[1], jnp.where(lanes[2], parts[2], parts[3])))

    return (gate[i, here, :] * (own_head(0) / own_head(WIDTH))).astype(bf16)


def send_block(at, step, block, blocks, send, recv, to_slots, send_sem, recv_sem):
    for g in range(2):
        part = jnp.concatenate([rows[g * 64 : (g + 1) * 64] for rows in blocks], axis=0)
        moved = jnp.dot(to_slots, part, preferred_element_type=f32).astype(bf16)
        send[pl.ds(block * 32 + g * 16, 16)] = moved.reshape(16, 16, C)
    me = slot_of(at)

    ys = [(at["y"] + by) % 4 for by in range(4)]
    xs = [(at["x"] + by) % 4 for by in range(4)]
    cores = [at["core"], 1 - at["core"]]

    def start(q):
        to = {"z": block, "y": ys[q // 8], "x": xs[q // 2 % 4], "core": cores[q % 2]}
        pltpu.make_async_remote_copy(
            src_ref=send.at[slot_of(to)],
            dst_ref=recv.at[me],
            send_sem=send_sem,
            recv_sem=recv_sem,
            device_id=device_of(to),
            device_id_type=MESH,
        ).start()

    for q in range(31, 0, -1):
        start(q)

    @pl.when(step < 3)
    def _():
        start(0)

    @pl.when(step == 3)
    def _():
        recv[me] = send[me]


def from_recv(recv, plane, to_rows):
    halves = []
    for g in range(2):
        part = recv[pl.ds(plane * 32 + g * 16, 16)].reshape(256, C)
        halves.append(jnp.dot(to_rows, part, preferred_element_type=f32).astype(bf16))
    return [jnp.concatenate([half[i * 64 : (i + 1) * 64] for half in halves], axis=0) for i in range(ROWS)]


def block_of(at, step):
    by = jnp.where(step == 0, STEPS[0], jnp.where(step == 1, STEPS[1], jnp.where(step == 2, STEPS[2], STEPS[3])))
    return (at["z"] + by) % 4


def kernel(
    pair_hbm,
    gain_s, shift_s, proj_s, bias_rows_s, gate_bias_s, out_weight_s, out_bias_s,
    gain_e, shift_e, proj_e, bias_rows_e, gate_bias_e, out_weight_e, out_bias_e,
    out_hbm,
    pair, normed, query, keys, values, gate, wide, raw, to_lanes,
    bias_s, bias_e, send_a, recv_a, send_b, recv_b,
    g_send_s, g_recv_s, g_send_e, g_recv_e, x_send, x_recv, in_sem, out_sem,
):
    at = where_am_i()
    barrier = pltpu.get_barrier_semaphore()
    greet = [shifted(at, axis, by) for axis in ("x", "y", "z") for by in (1, 2, 3)] + [shifted(at, "core", 1)]
    for one, two in (("x", "y"), ("x", "z"), ("y", "z")):
        greet += [shifted(shifted(at, one, i), two, j) for i in (1, 2, 3) for j in (1, 2, 3)]
    for other in greet:
        pl.semaphore_signal(barrier, inc=1, device_id=device_of(other), device_id_type=MESH)

    z, y, x, core = at["z"], slot_y(at["y"]), at["x"], at["core"]
    vec = lambda ref: ref[...].reshape(1, C)
    loads = [pltpu.make_async_copy(pair_hbm.at[i], pair.at[i], in_sem.at[i]) for i in range(ROWS)]
    for load in loads:
        load.start()
    for i in range(ROWS):
        loads[i].wait()
        normed[i] = layer_norm(pair[i], vec(gain_s), vec(shift_s))
    bias_s[z, y, x, core] = bias_slab(normed, bias_rows_s[...])
    pl.semaphore_wait(barrier, len(greet))
    for chunk in range(4):
        gather_plane(bias_s, at, chunk, g_send_s, g_recv_s)
    for i in range(ROWS):
        project(i, slice(None), normed[i], proj_s[...], vec(gate_bias_s), query, keys, values, gate)
    for block in range(2):
        pre_scores(block, query, keys, raw)
    gather_line(bias_s, at, range(4), g_send_s, g_recv_s, recv_a)
    for block in range(2, 4):
        pre_scores(block, query, keys, raw)
    to_rows, to_slots = perms()
    to_lanes[...] = lane_perm()
    for chunk in range(4):
        gather_core(bias_s, at, chunk, g_send_s, g_recv_s, recv_a)
    for chunk in range(4):
        gather_end(at, chunk, g_send_s, g_recv_s, recv_a)
        spread_start(bias_s, wide, to_rows, chunk)

    def start_step(step, carry):
        block = block_of(at, step)
        here = pl.ds(pl.multiple_of(block * 128, 128), 128)
        gated = [attention_block(i, block, raw, wide, values, gate) for i in range(ROWS)]
        update = jnp.dot(jnp.concatenate(gated, axis=0), out_weight_s[...], preferred_element_type=f32)
        after = pair[:, here, :].reshape(ROWS * 128, C) + update + vec(out_bias_s)
        pair[:, here, :] = after.reshape(ROWS, 128, C)
        ended = layer_norm(after, vec(gain_e), vec(shift_e))
        blocks = [ended[i * 128 : (i + 1) * 128] for i in range(ROWS)]
        slab = bias_slab(blocks, bias_rows_e[...])
        for s in range(4):

            @pl.when(step == s)
            def _(s=s):
                bias_e[z, y, x, core, :, s * 128 : (s + 1) * 128] = slab
                gather_plane(bias_e, at, s, g_send_e, g_recv_e)
                if s >= 2:
                    gather_line(bias_e, at, (s - 2,), g_send_e, g_recv_e, recv_b)

        send_block(at, step, block, blocks, send_a, recv_a, to_slots, x_send.at[0, step], x_recv.at[0, step])
        return carry

    lax.fori_loop(0, 4, start_step, 0)

    def receive(step):
        plane = (z + 4 - STEPS[step]) % 4
        wait_for(recv_a, 32 if step < 3 else 31, at, x_send.at[0, step], x_recv.at[0, step], False)
        here = pl.ds(pl.multiple_of(plane * 128, 128), 128)
        for i, rows in enumerate(from_recv(recv_a, plane, to_rows)):
            project(i, here, rows, proj_e[...], vec(gate_bias_e), query, keys, values, gate)

    def settle(chunk):
        gather_end(at, chunk, g_send_e, g_recv_e, recv_b)
        spread_end(bias_e, wide, to_lanes[...], chunk)

    receive(0)
    receive(1)
    gather_line(bias_e, at, (2,), g_send_e, g_recv_e, recv_b)
    for chunk in (0, 1):
        gather_core(bias_e, at, chunk, g_send_e, g_recv_e, recv_b)
    receive(2)
    gather_line(bias_e, at, (3,), g_send_e, g_recv_e, recv_b)
    receive(3)
    for block in range(2):
        pre_scores(block, query, keys, raw)
    gather_core(bias_e, at, 2, g_send_e, g_recv_e, recv_b)
    settle(0)
    settle(1)
    for block in range(2, 4):
        pre_scores(block, query, keys, raw)
    gather_core(bias_e, at, 3, g_send_e, g_recv_e, recv_b)
    settle(2)
    settle(3)

    def end_step(step, carry):
        block = block_of(at, step)
        blocks = [attention_block(i, block, raw, wide, values, gate) for i in range(ROWS)]
        send_block(at, step, block, blocks, send_b, recv_b, to_slots, x_send.at[1, step], x_recv.at[1, step])
        return carry

    lax.fori_loop(0, 4, end_step, 0)
    gather_drain(at, g_send_s, g_recv_s, recv_a)
    gather_drain(at, g_send_e, g_recv_e, recv_a)
    stores = []
    for step in range(4):
        plane = (z + 4 - STEPS[step]) % 4
        here = pl.ds(pl.multiple_of(plane * 128, 128), 128)
        wait_for(recv_b, 32 if step < 3 else 31, at, x_send.at[1, step], x_recv.at[1, step], False)
        for i, rows in enumerate(from_recv(recv_b, plane, to_rows)):
            update = jnp.dot(rows, out_weight_e[...], preferred_element_type=f32)
            pair[i, here, :] = pair[i, here, :] + update + vec(out_bias_e)
        stores.append(pltpu.make_async_copy(pair.at[:, here], out_hbm.at[:, here], out_sem.at[step]))
        stores[-1].start()
    for trip in range(2):
        for step in range(4):
            wait_for(recv_a, 32 if step < 3 else 31, at, x_send.at[trip, step], x_recv.at[trip, step], True)
    for store in stores:
        store.wait()


def body(*args):
    args = [arg.T if arg.shape == (C, H) else arg for arg in args]
    vmem = pl.BlockSpec(memory_space=pltpu.VMEM)
    slab = (4, 4, 4, 2, 16, N)
    return pl.pallas_call(
        kernel,
        out_shape=jax.ShapeDtypeStruct((ROWS, N, C), f32),
        in_specs=[pl.BlockSpec(memory_space=pl.ANY)] + [vmem] * (len(args) - 1),
        out_specs=pl.BlockSpec(memory_space=pl.ANY),
        scratch_shapes=[
            pltpu.VMEM((ROWS, N, C), f32),
            pltpu.VMEM((ROWS, N, C), bf16),
            pltpu.VMEM((ROWS, N, C), bf16),
            pltpu.VMEM((ROWS, N, C), bf16),
            pltpu.VMEM((ROWS, N, C), bf16),
            pltpu.VMEM((ROWS, N, C), f32),
            pltpu.VMEM((4, H * 128, N), f32),
            pltpu.VMEM((4, ROWS, H * 128, N), f32),
            pltpu.VMEM((512, 512), bf16),
            pltpu.VMEM(slab, bf16),
            pltpu.VMEM(slab, bf16),
            pltpu.VMEM((DEV, 16, C), bf16),
            pltpu.VMEM((DEV, 16, C), bf16),
            pltpu.VMEM((DEV, 16, C), bf16),
            pltpu.VMEM((DEV, 16, C), bf16),
            pltpu.SemaphoreType.DMA((4, 8)),
            pltpu.SemaphoreType.DMA((4, 8)),
            pltpu.SemaphoreType.DMA((4, 8)),
            pltpu.SemaphoreType.DMA((4, 8)),
            pltpu.SemaphoreType.DMA((2, 4)),
            pltpu.SemaphoreType.DMA((2, 4)),
            pltpu.SemaphoreType.DMA((4,)),
            pltpu.SemaphoreType.DMA((4,)),
        ],
        compiler_params=pltpu.CompilerParams(
            collective_id=0, has_side_effects=True, vmem_limit_bytes=56 << 20
        ),
    )(*args)


def solution(mesh):
    rows = P(("rb", "cb"), None, None)
    return jax.shard_map(body, mesh=mesh, in_specs=(rows,) + (P(),) * 14, out_specs=rows, check_vma=False)
```

```python
import functools

import jax
import jax.numpy as jnp
from jax import lax
from jax.experimental import pallas as pl
from jax.experimental.pallas import tpu as pltpu
from jax.sharding import PartitionSpec as P

H = 4
HEAD = 32
WIDTH = H * HEAD
ROWS = 4
N = 512
C = 128
DEV = 128
MESH = pl.DeviceIdType.MESH
f32 = jnp.float32
bf16 = jnp.bfloat16

LINES = (("z", "x", "y", "x"), ("z", "x", "y", "z"))
STEPS = (2, 1, 3, 0)


def where_am_i():
    rb, cb = lax.axis_index("rb"), lax.axis_index("cb")
    return {
        "z": rb // 4,
        "y": (cb % 2) * 2 + (rb // 2) % 2,
        "x": cb // 2,
        "core": rb % 2,
    }


def device_of(at):
    return (at["z"] * 4 + (at["y"] % 2) * 2 + at["core"], at["x"] * 2 + at["y"] // 2)


def slot_y(y):
    return (y % 2) * 2 + y // 2


def slot_of(at):
    return at["z"] * 32 + slot_y(at["y"]) * 8 + at["x"] * 2 + at["core"]


def shifted(at, axis, by):
    size = 2 if axis == "core" else 4
    return {**at, axis: (at[axis] + by) % size}


def perms():
    row = lax.broadcasted_iota(jnp.int32, (256, 256), 0)
    col = lax.broadcasted_iota(jnp.int32, (256, 256), 1)

    def slot(n):
        return (n % 2) * 8 + ((n // 2) % 4) * 2 + n // 8

    a, n, b = row // 64, (row // 4) % 16, row % 4
    to_rows = jnp.where(col == slot(n) * 16 + a * 4 + b, 1.0, 0.0).astype(bf16)
    a, n, b = col // 64, (col // 4) % 16, col % 4
    to_slots = jnp.where(row == slot(n) * 16 + b * 4 + a, 1.0, 0.0).astype(bf16)
    return to_rows, to_slots


def lane_perm():
    row = lax.broadcasted_iota(jnp.int32, (512, 512), 0)
    col = lax.broadcasted_iota(jnp.int32, (512, 512), 1)
    a, n, b = col // 128, (col // 4) % 32, col % 4
    slot = n // 16 * 16 + (n % 2) * 8 + ((n // 2) % 4) * 2 + (n // 8) % 2
    return jnp.where(row == slot * 16 + a * 4 + b, 1.0, 0.0).astype(bf16)


def layer_norm(pair, gain, shift):
    mean = jnp.mean(pair, axis=-1, keepdims=True)
    away = pair - mean
    varia = jnp.mean(away * away, axis=-1, keepdims=True)
    return (away / jnp.sqrt(varia + 1e-05) * gain + shift).astype(bf16)


def bias_slab(normed, bias_rows):
    pick = lax.broadcasted_iota(jnp.int32, (16, H), 0) // 4 == lax.broadcasted_iota(jnp.int32, (16, H), 1)
    wide = jnp.dot(jnp.where(pick, 1.0, 0.0).astype(bf16), bias_rows, preferred_element_type=f32)
    row = lax.broadcasted_iota(jnp.int32, (16, C), 0) % 4
    total = None
    for i in range(ROWS):
        mine = jnp.where(row == i, wide, 0.0).astype(bf16)
        part = lax.dot_general(mine, normed[i], (((1,), (1,)), ((), ())), preferred_element_type=f32)
        total = part if total is None else total + part
    return total.astype(bf16)


def tiles(ref, count):
    return ref.at[pl.ds(0, count)]


def wait_for(ref, count, at, send_sem, recv_sem, sent):
    part = tiles(ref, count)
    copy = pltpu.make_async_remote_copy(
        src_ref=part,
        dst_ref=part,
        send_sem=send_sem,
        recv_sem=recv_sem,
        device_id=device_of(shifted(at, "core", 1)),
        device_id_type=MESH,
    )
    if sent:
        copy.wait_send()
    else:
        copy.wait_recv()


def part_of(bias, at, chunk, whole):
    all4 = pl.ds(0, 4)
    return bias.at[
        all4 if "z" in whole else at["z"],
        all4 if "y" in whole else slot_y(at["y"]),
        all4 if "x" in whole else at["x"],
        at["core"],
        :,
        pl.ds(chunk * 128, 128),
    ]


def push(part, to, send_sem, recv_sem):
    pltpu.make_async_remote_copy(
        src_ref=part,
        dst_ref=part,
        send_sem=send_sem,
        recv_sem=recv_sem,
        device_id=device_of(to),
        device_id_type=MESH,
    ).start()


def along(at, chunk, act):
    lines = [core_lines[chunk] for core_lines in LINES]
    for core, line in enumerate(lines):
        if core == 1 and lines[0] == lines[1]:
            continue
        plane = [axis for axis in ("z", "y", "x") if axis != line]
        if lines[0] == lines[1]:
            act(line, plane)
        else:
            pl.when(at["core"] == core)(functools.partial(act, line, plane))


def gather_plane(bias, at, chunk, send_sem, recv_sem):
    part = part_of(bias, at, chunk, ())

    def act(line, plane):
        for one in (2, 1, 3, 0):
            for two in (2, 1, 3, 0):
                if one or two:
                    to = shifted(shifted(at, plane[0], one), plane[1], two)
                    push(part, to, send_sem.at[chunk, one], recv_sem.at[chunk, one])

    along(at, chunk, act)


def gather_row(bias, at, chunk, one, send_sem, recv_sem, spare):
    wait_for(spare, 4 if one else 3, at, send_sem.at[chunk, one], recv_sem.at[chunk, one], False)

    def act(line, plane):
        part = part_of(bias, shifted(at, plane[0], 4 - one), chunk, plane[1:])
        for by in (2, 1, 3):
            push(part, shifted(at, line, by), send_sem.at[chunk, 4 + by], recv_sem.at[chunk, 4 + by])

    along(at, chunk, act)


def gather_line(bias, at, chunks, send_sem, recv_sem, spare):
    for one in (0, 1, 3, 2):
        for chunk in chunks:
            gather_row(bias, at, chunk, one, send_sem, recv_sem, spare)
    for chunk in chunks:
        along(
            at,
            chunk,
            lambda line, plane, chunk=chunk: push(
                part_of(bias, at, chunk, plane), shifted(at, "core", 1), send_sem.at[chunk, 4], recv_sem.at[chunk, 4]
            ),
        )


def gather_core(bias, at, chunk, send_sem, recv_sem, spare):
    def act(line, plane):
        for by in (1, 3, 2):
            wait_for(spare, 16, at, send_sem.at[chunk, 4 + by], recv_sem.at[chunk, 4 + by], False)
            part = part_of(bias, shifted(at, line, 4 - by), chunk, plane)
            push(part, shifted(at, "core", 1), send_sem.at[chunk, 4], recv_sem.at[chunk, 4])

    along(at, chunk, act)


def gather_end(at, chunk, send_sem, recv_sem, spare):
    wait_for(spare, 64, at, send_sem.at[chunk, 4], recv_sem.at[chunk, 4], False)


def gather_drain(at, send_sem, recv_sem, spare):
    for chunk in range(4):
        for phase, count in ((0, 3), (1, 4), (2, 4), (3, 4), (4, 64), (5, 16), (6, 16), (7, 16)):
            wait_for(spare, count, at, send_sem.at[chunk, phase], recv_sem.at[chunk, phase], True)


def spread_start(bias, wide, to_rows, chunk):
    here = slice(chunk * 128, (chunk + 1) * 128)
    for z in range(4):
        for y in range(2):
            slabs = bias[z, 2 * y : 2 * y + 2, :, :, :, here].reshape(256, 128)
            rows = jnp.dot(to_rows, slabs, preferred_element_type=f32)
            for h in range(H):
                first = h * 128 + y * 64
                wide[z, first : first + 64, here] = rows[h * 64 : (h + 1) * 64]


def spread_end(bias, wide, to_lanes, step):
    for z in range(4):
        block = (z + STEPS[step]) % 4
        slabs = bias[z, :, :, :, :, step * 128 : (step + 1) * 128].reshape(512, 128)
        cols = lax.dot_general(slabs, to_lanes, (((0,), (0,)), ((), ())), preferred_element_type=f32)
        for h in range(H):
            wide[block, h * 128 : (h + 1) * 128, z * 128 : (z + 1) * 128] = cols[:, h * 128 : (h + 1) * 128]


def project(i, here, rows, proj, gate_bias, query, keys, values, gate):
    out = jnp.dot(rows, proj, preferred_element_type=f32)
    query[i, here, :] = (out[:, :WIDTH] / jnp.sqrt(f32(HEAD))).astype(bf16)
    keys[i, here, :] = out[:, WIDTH : 2 * WIDTH].astype(bf16)
    values[i, here, :] = out[:, 2 * WIDTH : 3 * WIDTH].astype(bf16)
    gate[i, here, :] = jax.nn.sigmoid(out[:, 3 * WIDTH :] + gate_bias)


def head_lanes(h, shape):
    return lax.broadcasted_iota(jnp.int32, shape, len(shape) - 1) // HEAD == h


def pre_scores(block, query, keys, raw):
    lanes = [head_lanes(h, (128, C)) for h in range(H)]
    for i in range(ROWS):
        q = query[i, pl.ds(pl.multiple_of(block * 128, 128), 128), :]
        q_heads = jnp.concatenate([jnp.where(lane, q, 0.0).astype(bf16) for lane in lanes], axis=0)
        raw[block, i] = lax.dot_general(q_heads, keys[i], (((1,), (1,)), ((), ())), preferred_element_type=f32)


def attention_block(i, block, raw, wide, values, gate):
    here = pl.ds(pl.multiple_of(block * 128, 128), 128)
    lanes = [head_lanes(h, (128, C)) for h in range(H)]
    scores = raw[block, i] + wide[block]
    top = jnp.max(scores, axis=-1, keepdims=True)
    weights = jnp.exp(scores - top).astype(bf16)
    v_ones = jnp.concatenate([values[i], jnp.ones((N, C), bf16)], axis=1)
    sums = jnp.dot(weights, v_ones, preferred_element_type=f32)

    def own_head(cols):
        parts = [sums[h * 128 : (h + 1) * 128, cols : cols + WIDTH] for h in range(H)]
        return jnp.where(lanes[0], parts[0], jnp.where(lanes[1], parts[1], jnp.where(lanes[2], parts[2], parts[3])))

    return (gate[i, here, :] * (own_head(0) / own_head(WIDTH))).astype(bf16)


def send_block(at, step, block, blocks, send, recv, to_slots, send_sem, recv_sem):
    for g in range(2):
        part = jnp.concatenate([rows[g * 64 : (g + 1) * 64] for rows in blocks], axis=0)
        moved = jnp.dot(to_slots, part, preferred_element_type=f32).astype(bf16)
        send[pl.ds(block * 32 + g * 16, 16)] = moved.reshape(16, 16, C)
    me = slot_of(at)

    ys = [(at["y"] + by) % 4 for by in range(4)]
    xs = [(at["x"] + by) % 4 for by in range(4)]
    cores = [at["core"], 1 - at["core"]]

    def start(q):
        to = {"z": block, "y": ys[q // 8], "x": xs[q // 2 % 4], "core": cores[q % 2]}
        pltpu.make_async_remote_copy(
            src_ref=send.at[slot_of(to)],
            dst_ref=recv.at[me],
            send_sem=send_sem,
            recv_sem=recv_sem,
            device_id=device_of(to),
            device_id_type=MESH,
        ).start()

    for q in range(31, 0, -1):
        start(q)

    @pl.when(step < 3)
    def _():
        start(0)

    @pl.when(step == 3)
    def _():
        recv[me] = send[me]


def from_recv(recv, plane, to_rows):
    halves = []
    for g in range(2):
        part = recv[pl.ds(plane * 32 + g * 16, 16)].reshape(256, C)
        halves.append(jnp.dot(to_rows, part, preferred_element_type=f32).astype(bf16))
    return [jnp.concatenate([half[i * 64 : (i + 1) * 64] for half in halves], axis=0) for i in range(ROWS)]


def block_of(at, step):
    by = jnp.where(step == 0, STEPS[0], jnp.where(step == 1, STEPS[1], jnp.where(step == 2, STEPS[2], STEPS[3])))
    return (at["z"] + by) % 4


def kernel(
    pair_hbm,
    gain_s, shift_s, proj_s, bias_rows_s, gate_bias_s, out_weight_s, out_bias_s,
    gain_e, shift_e, proj_e, bias_rows_e, gate_bias_e, out_weight_e, out_bias_e,
    out_hbm,
    pair, normed, query, keys, values, gate, wide, raw, to_lanes,
    bias_s, bias_e, send_a, recv_a, send_b, recv_b,
    g_send_s, g_recv_s, g_send_e, g_recv_e, x_send, x_recv, in_sem, out_sem,
):
    at = where_am_i()
    barrier = pltpu.get_barrier_semaphore()
    greet = [shifted(at, axis, by) for axis in ("x", "y", "z") for by in (1, 2, 3)] + [shifted(at, "core", 1)]
    for one, two in (("x", "y"), ("x", "z"), ("y", "z")):
        greet += [shifted(shifted(at, one, i), two, j) for i in (1, 2, 3) for j in (1, 2, 3)]
    for other in greet:
        pl.semaphore_signal(barrier, inc=1, device_id=device_of(other), device_id_type=MESH)

    z, y, x, core = at["z"], slot_y(at["y"]), at["x"], at["core"]
    vec = lambda ref: ref[...].reshape(1, C)
    loads = [pltpu.make_async_copy(pair_hbm.at[i], pair.at[i], in_sem.at[i]) for i in range(ROWS)]
    for load in loads:
        load.start()
    for i in range(ROWS):
        loads[i].wait()
        normed[i] = layer_norm(pair[i], vec(gain_s), vec(shift_s))
    bias_s[z, y, x, core] = bias_slab(normed, bias_rows_s[...])
    pl.semaphore_wait(barrier, len(greet))
    for chunk in range(4):
        gather_plane(bias_s, at, chunk, g_send_s, g_recv_s)
    for i in range(ROWS):
        project(i, slice(None), normed[i], proj_s[...], vec(gate_bias_s), query, keys, values, gate)
    for block in range(2):
        pre_scores(block, query, keys, raw)
    gather_line(bias_s, at, range(4), g_send_s, g_recv_s, recv_a)
    for block in range(2, 4):
        pre_scores(block, query, keys, raw)
    to_rows, to_slots = perms()
    to_lanes[...] = lane_perm()
    for chunk in range(4):
        gather_core(bias_s, at, chunk, g_send_s, g_recv_s, recv_a)
    for chunk in range(4):
        gather_end(at, chunk, g_send_s, g_recv_s, recv_a)
        spread_start(bias_s, wide, to_rows, chunk)

    def start_step(step, carry):
        block = block_of(at, step)
        here = pl.ds(pl.multiple_of(block * 128, 128), 128)
        gated = [attention_block(i, block, raw, wide, values, gate) for i in range(ROWS)]
        update = jnp.dot(jnp.concatenate(gated, axis=0), out_weight_s[...], preferred_element_type=f32)
        after = pair[:, here, :].reshape(ROWS * 128, C) + update + vec(out_bias_s)
        pair[:, here, :] = after.reshape(ROWS, 128, C)
        ended = layer_norm(after, vec(gain_e), vec(shift_e))
        blocks = [ended[i * 128 : (i + 1) * 128] for i in range(ROWS)]
        slab = bias_slab(blocks, bias_rows_e[...])
        for s in range(4):

            @pl.when(step == s)
            def _(s=s):
                bias_e[z, y, x, core, :, s * 128 : (s + 1) * 128] = slab
                gather_plane(bias_e, at, s, g_send_e, g_recv_e)
                if s >= 2:
                    gather_line(bias_e, at, (s - 2,), g_send_e, g_recv_e, recv_b)

        send_block(at, step, block, blocks, send_a, recv_a, to_slots, x_send.at[0, step], x_recv.at[0, step])
        return carry

    lax.fori_loop(0, 4, start_step, 0)

    def receive(step):
        plane = (z + 4 - STEPS[step]) % 4
        wait_for(recv_a, 32 if step < 3 else 31, at, x_send.at[0, step], x_recv.at[0, step], False)
        here = pl.ds(pl.multiple_of(plane * 128, 128), 128)
        for i, rows in enumerate(from_recv(recv_a, plane, to_rows)):
            project(i, here, rows, proj_e[...], vec(gate_bias_e), query, keys, values, gate)

    def settle(chunk):
        gather_end(at, chunk, g_send_e, g_recv_e, recv_b)
        spread_end(bias_e, wide, to_lanes[...], chunk)

    receive(0)
    receive(1)
    gather_line(bias_e, at, (2,), g_send_e, g_recv_e, recv_b)
    gather_core(bias_e, at, 0, g_send_e, g_recv_e, recv_b)
    gather_core(bias_e, at, 1, g_send_e, g_recv_e, recv_b)
    receive(2)
    gather_line(bias_e, at, (3,), g_send_e, g_recv_e, recv_b)
    settle(0)
    settle(1)
    receive(3)
    pre_scores(0, query, keys, raw)
    gather_core(bias_e, at, 2, g_send_e, g_recv_e, recv_b)
    pre_scores(1, query, keys, raw)
    pre_scores(2, query, keys, raw)
    gather_core(bias_e, at, 3, g_send_e, g_recv_e, recv_b)
    settle(2)
    pre_scores(3, query, keys, raw)
    settle(3)

    def end_step(step, carry):
        block = block_of(at, step)
        blocks = [attention_block(i, block, raw, wide, values, gate) for i in range(ROWS)]
        send_block(at, step, block, blocks, send_b, recv_b, to_slots, x_send.at[1, step], x_recv.at[1, step])
        return carry

    lax.fori_loop(0, 4, end_step, 0)
    gather_drain(at, g_send_s, g_recv_s, recv_a)
    gather_drain(at, g_send_e, g_recv_e, recv_a)
    stores = []
    for step in range(4):
        plane = (z + 4 - STEPS[step]) % 4
        here = pl.ds(pl.multiple_of(plane * 128, 128), 128)
        wait_for(recv_b, 32 if step < 3 else 31, at, x_send.at[1, step], x_recv.at[1, step], False)
        for i, rows in enumerate(from_recv(recv_b, plane, to_rows)):
            update = jnp.dot(rows, out_weight_e[...], preferred_element_type=f32)
            pair[i, here, :] = pair[i, here, :] + update + vec(out_bias_e)
        stores.append(pltpu.make_async_copy(pair.at[:, here], out_hbm.at[:, here], out_sem.at[step]))
        stores[-1].start()
    for trip in range(2):
        for step in range(4):
            wait_for(recv_a, 32 if step < 3 else 31, at, x_send.at[trip, step], x_recv.at[trip, step], True)
    for store in stores:
        store.wait()


def body(*args):
    args = [arg.T if arg.shape == (C, H) else arg for arg in args]
    vmem = pl.BlockSpec(memory_space=pltpu.VMEM)
    slab = (4, 4, 4, 2, 16, N)
    return pl.pallas_call(
        kernel,
        out_shape=jax.ShapeDtypeStruct((ROWS, N, C), f32),
        in_specs=[pl.BlockSpec(memory_space=pl.ANY)] + [vmem] * (len(args) - 1),
        out_specs=pl.BlockSpec(memory_space=pl.ANY),
        scratch_shapes=[
            pltpu.VMEM((ROWS, N, C), f32),
            pltpu.VMEM((ROWS, N, C), bf16),
            pltpu.VMEM((ROWS, N, C), bf16),
            pltpu.VMEM((ROWS, N, C), bf16),
            pltpu.VMEM((ROWS, N, C), bf16),
            pltpu.VMEM((ROWS, N, C), f32),
            pltpu.VMEM((4, H * 128, N), f32),
            pltpu.VMEM((4, ROWS, H * 128, N), f32),
            pltpu.VMEM((512, 512), bf16),
            pltpu.VMEM(slab, bf16),
            pltpu.VMEM(slab, bf16),
            pltpu.VMEM((DEV, 16, C), bf16),
            pltpu.VMEM((DEV, 16, C), bf16),
            pltpu.VMEM((DEV, 16, C), bf16),
            pltpu.VMEM((DEV, 16, C), bf16),
            pltpu.SemaphoreType.DMA((4, 8)),
            pltpu.SemaphoreType.DMA((4, 8)),
            pltpu.SemaphoreType.DMA((4, 8)),
            pltpu.SemaphoreType.DMA((4, 8)),
            pltpu.SemaphoreType.DMA((2, 4)),
            pltpu.SemaphoreType.DMA((2, 4)),
            pltpu.SemaphoreType.DMA((4,)),
            pltpu.SemaphoreType.DMA((4,)),
        ],
        compiler_params=pltpu.CompilerParams(
            collective_id=0, has_side_effects=True, vmem_limit_bytes=56 << 20
        ),
    )(*args)


def solution(mesh):
    rows = P(("rb", "cb"), None, None)
    return jax.shard_map(body, mesh=mesh, in_specs=(rows,) + (P(),) * 14, out_specs=rows, check_vma=False)
```

```python
import functools

import jax
import jax.numpy as jnp
from jax import lax
from jax.experimental import pallas as pl
from jax.experimental.pallas import tpu as pltpu
from jax.sharding import PartitionSpec as P

H = 4
HEAD = 32
WIDTH = H * HEAD
ROWS = 4
N = 512
C = 128
DEV = 128
MESH = pl.DeviceIdType.MESH
f32 = jnp.float32
bf16 = jnp.bfloat16

LINES = (("z", "x", "y", "x"), ("z", "x", "y", "z"))
STEPS = (2, 1, 3, 0)


def where_am_i():
    rb, cb = lax.axis_index("rb"), lax.axis_index("cb")
    return {
        "z": rb // 4,
        "y": (cb % 2) * 2 + (rb // 2) % 2,
        "x": cb // 2,
        "core": rb % 2,
    }


def device_of(at):
    return (at["z"] * 4 + (at["y"] % 2) * 2 + at["core"], at["x"] * 2 + at["y"] // 2)


def slot_y(y):
    return (y % 2) * 2 + y // 2


def slot_of(at):
    return at["z"] * 32 + slot_y(at["y"]) * 8 + at["x"] * 2 + at["core"]


def shifted(at, axis, by):
    size = 2 if axis == "core" else 4
    return {**at, axis: (at[axis] + by) % size}


def perms():
    row = lax.broadcasted_iota(jnp.int32, (256, 256), 0)
    col = lax.broadcasted_iota(jnp.int32, (256, 256), 1)

    def slot(n):
        return (n % 2) * 8 + ((n // 2) % 4) * 2 + n // 8

    a, n, b = row // 64, (row // 4) % 16, row % 4
    to_rows = jnp.where(col == slot(n) * 16 + a * 4 + b, 1.0, 0.0).astype(bf16)
    a, n, b = col // 64, (col // 4) % 16, col % 4
    to_slots = jnp.where(row == slot(n) * 16 + b * 4 + a, 1.0, 0.0).astype(bf16)
    return to_rows, to_slots


def lane_perm():
    row = lax.broadcasted_iota(jnp.int32, (512, 512), 0)
    col = lax.broadcasted_iota(jnp.int32, (512, 512), 1)
    a, n, b = col // 128, (col // 4) % 32, col % 4
    slot = n // 16 * 16 + (n % 2) * 8 + ((n // 2) % 4) * 2 + (n // 8) % 2
    return jnp.where(row == slot * 16 + a * 4 + b, 1.0, 0.0).astype(bf16)


def layer_norm(pair, gain, shift):
    mean = jnp.mean(pair, axis=-1, keepdims=True)
    away = pair - mean
    varia = jnp.mean(away * away, axis=-1, keepdims=True)
    return (away / jnp.sqrt(varia + 1e-05) * gain + shift).astype(bf16)


def bias_slab(normed, bias_rows):
    pick = lax.broadcasted_iota(jnp.int32, (16, H), 0) // 4 == lax.broadcasted_iota(jnp.int32, (16, H), 1)
    wide = jnp.dot(jnp.where(pick, 1.0, 0.0).astype(bf16), bias_rows, preferred_element_type=f32)
    row = lax.broadcasted_iota(jnp.int32, (16, C), 0) % 4
    total = None
    for i in range(ROWS):
        mine = jnp.where(row == i, wide, 0.0).astype(bf16)
        part = lax.dot_general(mine, normed[i], (((1,), (1,)), ((), ())), preferred_element_type=f32)
        total = part if total is None else total + part
    return total.astype(bf16)


def tiles(ref, count):
    return ref.at[pl.ds(0, count)]


def wait_for(ref, count, at, send_sem, recv_sem, sent):
    part = tiles(ref, count)
    copy = pltpu.make_async_remote_copy(
        src_ref=part,
        dst_ref=part,
        send_sem=send_sem,
        recv_sem=recv_sem,
        device_id=device_of(shifted(at, "core", 1)),
        device_id_type=MESH,
    )
    if sent:
        copy.wait_send()
    else:
        copy.wait_recv()


def part_of(bias, at, chunk, whole):
    all4 = pl.ds(0, 4)
    return bias.at[
        all4 if "z" in whole else at["z"],
        all4 if "y" in whole else slot_y(at["y"]),
        all4 if "x" in whole else at["x"],
        at["core"],
        :,
        pl.ds(chunk * 128, 128),
    ]


def push(part, to, send_sem, recv_sem):
    pltpu.make_async_remote_copy(
        src_ref=part,
        dst_ref=part,
        send_sem=send_sem,
        recv_sem=recv_sem,
        device_id=device_of(to),
        device_id_type=MESH,
    ).start()


def along(at, chunk, act):
    lines = [core_lines[chunk] for core_lines in LINES]
    for core, line in enumerate(lines):
        if core == 1 and lines[0] == lines[1]:
            continue
        plane = [axis for axis in ("z", "y", "x") if axis != line]
        if lines[0] == lines[1]:
            act(line, plane)
        else:
            pl.when(at["core"] == core)(functools.partial(act, line, plane))


def gather_plane(bias, at, chunk, send_sem, recv_sem):
    part = part_of(bias, at, chunk, ())

    def act(line, plane):
        for one in (2, 1, 3, 0):
            for two in (2, 1, 3, 0):
                if one or two:
                    to = shifted(shifted(at, plane[0], one), plane[1], two)
                    push(part, to, send_sem.at[chunk, one], recv_sem.at[chunk, one])

    along(at, chunk, act)


def gather_row(bias, at, chunk, one, send_sem, recv_sem, spare):
    wait_for(spare, 4 if one else 3, at, send_sem.at[chunk, one], recv_sem.at[chunk, one], False)

    def act(line, plane):
        part = part_of(bias, shifted(at, plane[0], 4 - one), chunk, plane[1:])
        for by in (2, 1, 3):
            push(part, shifted(at, line, by), send_sem.at[chunk, 4 + by], recv_sem.at[chunk, 4 + by])

    along(at, chunk, act)


def gather_line(bias, at, chunks, send_sem, recv_sem, spare):
    for one in (0, 1, 3, 2):
        for chunk in chunks:
            gather_row(bias, at, chunk, one, send_sem, recv_sem, spare)
    for chunk in chunks:
        along(
            at,
            chunk,
            lambda line, plane, chunk=chunk: push(
                part_of(bias, at, chunk, plane), shifted(at, "core", 1), send_sem.at[chunk, 4], recv_sem.at[chunk, 4]
            ),
        )


def gather_core(bias, at, chunk, send_sem, recv_sem, spare):
    def act(line, plane):
        for by in (1, 3, 2):
            wait_for(spare, 16, at, send_sem.at[chunk, 4 + by], recv_sem.at[chunk, 4 + by], False)
            part = part_of(bias, shifted(at, line, 4 - by), chunk, plane)
            push(part, shifted(at, "core", 1), send_sem.at[chunk, 4], recv_sem.at[chunk, 4])

    along(at, chunk, act)


def gather_end(at, chunk, send_sem, recv_sem, spare):
    wait_for(spare, 64, at, send_sem.at[chunk, 4], recv_sem.at[chunk, 4], False)


def gather_drain(at, send_sem, recv_sem, spare):
    for chunk in range(4):
        for phase, count in ((0, 3), (1, 4), (2, 4), (3, 4), (4, 64), (5, 16), (6, 16), (7, 16)):
            wait_for(spare, count, at, send_sem.at[chunk, phase], recv_sem.at[chunk, phase], True)


def spread_start(bias, wide, to_rows, chunk):
    here = slice(chunk * 128, (chunk + 1) * 128)
    for z in range(4):
        for y in range(2):
            slabs = bias[z, 2 * y : 2 * y + 2, :, :, :, here].reshape(256, 128)
            rows = jnp.dot(to_rows, slabs, preferred_element_type=f32)
            for h in range(H):
                first = h * 128 + y * 64
                wide[z, first : first + 64, here] = rows[h * 64 : (h + 1) * 64]


def spread_end(bias, wide, to_lanes, step):
    for z in range(4):
        block = (z + STEPS[step]) % 4
        slabs = bias[z, :, :, :, :, step * 128 : (step + 1) * 128].reshape(512, 128)
        cols = lax.dot_general(slabs, to_lanes, (((0,), (0,)), ((), ())), preferred_element_type=f32)
        for h in range(H):
            wide[block, h * 128 : (h + 1) * 128, z * 128 : (z + 1) * 128] = cols[:, h * 128 : (h + 1) * 128]


def project(i, here, rows, proj, gate_bias, query, keys, values, gate):
    out = jnp.dot(rows, proj, preferred_element_type=f32)
    query[i, here, :] = (out[:, :WIDTH] / jnp.sqrt(f32(HEAD))).astype(bf16)
    keys[i, here, :] = out[:, WIDTH : 2 * WIDTH].astype(bf16)
    values[i, here, :] = out[:, 2 * WIDTH : 3 * WIDTH].astype(bf16)
    gate[i, here, :] = jax.nn.sigmoid(out[:, 3 * WIDTH :] + gate_bias)


def head_lanes(h, shape):
    return lax.broadcasted_iota(jnp.int32, shape, len(shape) - 1) // HEAD == h


def pre_scores(block, query, keys, raw):
    lanes = [head_lanes(h, (128, C)) for h in range(H)]
    for i in range(ROWS):
        q = query[i, pl.ds(pl.multiple_of(block * 128, 128), 128), :]
        q_heads = jnp.concatenate([jnp.where(lane, q, 0.0).astype(bf16) for lane in lanes], axis=0)
        raw[block, i] = lax.dot_general(q_heads, keys[i], (((1,), (1,)), ((), ())), preferred_element_type=f32)


def attention_block(i, block, raw, wide, values, gate):
    here = pl.ds(pl.multiple_of(block * 128, 128), 128)
    lanes = [head_lanes(h, (128, C)) for h in range(H)]
    scores = raw[block, i] + wide[block]
    top = jnp.max(scores, axis=-1, keepdims=True)
    weights = jnp.exp(scores - top).astype(bf16)
    v_ones = jnp.concatenate([values[i], jnp.ones((N, C), bf16)], axis=1)
    sums = jnp.dot(weights, v_ones, preferred_element_type=f32)

    def own_head(cols):
        parts = [sums[h * 128 : (h + 1) * 128, cols : cols + WIDTH] for h in range(H)]
        return jnp.where(lanes[0], parts[0], jnp.where(lanes[1], parts[1], jnp.where(lanes[2], parts[2], parts[3])))

    return (gate[i, here, :] * (own_head(0) / own_head(WIDTH))).astype(bf16)


def send_block(at, step, block, blocks, send, recv, to_slots, send_sem, recv_sem):
    for g in range(2):
        part = jnp.concatenate([rows[g * 64 : (g + 1) * 64] for rows in blocks], axis=0)
        moved = jnp.dot(to_slots, part, preferred_element_type=f32).astype(bf16)
        send[pl.ds(block * 32 + g * 16, 16)] = moved.reshape(16, 16, C)
    me = slot_of(at)

    ys = [(at["y"] + by) % 4 for by in range(4)]
    xs = [(at["x"] + by) % 4 for by in range(4)]
    cores = [at["core"], 1 - at["core"]]

    def start(q):
        to = {"z": block, "y": ys[q // 8], "x": xs[q // 2 % 4], "core": cores[q % 2]}
        pltpu.make_async_remote_copy(
            src_ref=send.at[slot_of(to)],
            dst_ref=recv.at[me],
            send_sem=send_sem,
            recv_sem=recv_sem,
            device_id=device_of(to),
            device_id_type=MESH,
        ).start()

    for q in range(31, 0, -1):
        start(q)

    @pl.when(step < 3)
    def _():
        start(0)

    @pl.when(step == 3)
    def _():
        recv[me] = send[me]


def from_recv(recv, plane, to_rows):
    halves = []
    for g in range(2):
        part = recv[pl.ds(plane * 32 + g * 16, 16)].reshape(256, C)
        halves.append(jnp.dot(to_rows, part, preferred_element_type=f32).astype(bf16))
    return [jnp.concatenate([half[i * 64 : (i + 1) * 64] for half in halves], axis=0) for i in range(ROWS)]


def block_of(at, step):
    by = jnp.where(step == 0, STEPS[0], jnp.where(step == 1, STEPS[1], jnp.where(step == 2, STEPS[2], STEPS[3])))
    return (at["z"] + by) % 4


def kernel(
    pair_hbm,
    gain_s, shift_s, proj_s, bias_rows_s, gate_bias_s, out_weight_s, out_bias_s,
    gain_e, shift_e, proj_e, bias_rows_e, gate_bias_e, out_weight_e, out_bias_e,
    out_hbm,
    pair, normed, query, keys, values, gate, wide, raw, to_lanes,
    bias_s, bias_e, send_a, recv_a, send_b, recv_b,
    g_send_s, g_recv_s, g_send_e, g_recv_e, x_send, x_recv, in_sem, out_sem,
):
    at = where_am_i()
    barrier = pltpu.get_barrier_semaphore()
    greet = [shifted(at, axis, by) for axis in ("x", "y", "z") for by in (1, 2, 3)] + [shifted(at, "core", 1)]
    for one, two in (("x", "y"), ("x", "z"), ("y", "z")):
        greet += [shifted(shifted(at, one, i), two, j) for i in (1, 2, 3) for j in (1, 2, 3)]
    for other in greet:
        pl.semaphore_signal(barrier, inc=1, device_id=device_of(other), device_id_type=MESH)

    z, y, x, core = at["z"], slot_y(at["y"]), at["x"], at["core"]
    vec = lambda ref: ref[...].reshape(1, C)
    loads = [pltpu.make_async_copy(pair_hbm.at[i], pair.at[i], in_sem.at[i]) for i in range(ROWS)]
    for load in loads:
        load.start()
    for i in range(ROWS):
        loads[i].wait()
        normed[i] = layer_norm(pair[i], vec(gain_s), vec(shift_s))
    bias_s[z, y, x, core] = bias_slab(normed, bias_rows_s[...])
    pl.semaphore_wait(barrier, len(greet))
    for chunk in range(4):
        gather_plane(bias_s, at, chunk, g_send_s, g_recv_s)
    for i in range(ROWS):
        project(i, slice(None), normed[i], proj_s[...], vec(gate_bias_s), query, keys, values, gate)
    for block in range(2):
        pre_scores(block, query, keys, raw)
    gather_line(bias_s, at, range(4), g_send_s, g_recv_s, recv_a)
    for block in range(2, 4):
        pre_scores(block, query, keys, raw)
    to_rows, to_slots = perms()
    to_lanes[...] = lane_perm()
    for chunk in range(5):
        if chunk < 4:
            gather_core(bias_s, at, chunk, g_send_s, g_recv_s, recv_a)
        if chunk > 0:
            gather_end(at, chunk - 1, g_send_s, g_recv_s, recv_a)
            spread_start(bias_s, wide, to_rows, chunk - 1)

    def start_step(step, carry):
        block = block_of(at, step)
        here = pl.ds(pl.multiple_of(block * 128, 128), 128)
        gated = [attention_block(i, block, raw, wide, values, gate) for i in range(ROWS)]
        update = jnp.dot(jnp.concatenate(gated, axis=0), out_weight_s[...], preferred_element_type=f32)
        after = pair[:, here, :].reshape(ROWS * 128, C) + update + vec(out_bias_s)
        pair[:, here, :] = after.reshape(ROWS, 128, C)
        ended = layer_norm(after, vec(gain_e), vec(shift_e))
        blocks = [ended[i * 128 : (i + 1) * 128] for i in range(ROWS)]
        slab = bias_slab(blocks, bias_rows_e[...])
        for s in range(4):

            @pl.when(step == s)
            def _(s=s):
                bias_e[z, y, x, core, :, s * 128 : (s + 1) * 128] = slab
                gather_plane(bias_e, at, s, g_send_e, g_recv_e)
                if s >= 2:
                    gather_line(bias_e, at, (s - 2,), g_send_e, g_recv_e, recv_b)

        send_block(at, step, block, blocks, send_a, recv_a, to_slots, x_send.at[0, step], x_recv.at[0, step])
        return carry

    lax.fori_loop(0, 4, start_step, 0)

    def receive(step):
        plane = (z + 4 - STEPS[step]) % 4
        wait_for(recv_a, 32 if step < 3 else 31, at, x_send.at[0, step], x_recv.at[0, step], False)
        here = pl.ds(pl.multiple_of(plane * 128, 128), 128)
        for i, rows in enumerate(from_recv(recv_a, plane, to_rows)):
            project(i, here, rows, proj_e[...], vec(gate_bias_e), query, keys, values, gate)

    def settle(chunk):
        gather_end(at, chunk, g_send_e, g_recv_e, recv_b)
        spread_end(bias_e, wide, to_lanes[...], chunk)

    receive(0)
    receive(1)
    gather_line(bias_e, at, (2,), g_send_e, g_recv_e, recv_b)
    gather_core(bias_e, at, 0, g_send_e, g_recv_e, recv_b)
    gather_core(bias_e, at, 1, g_send_e, g_recv_e, recv_b)
    receive(2)
    gather_line(bias_e, at, (3,), g_send_e, g_recv_e, recv_b)
    settle(0)
    settle(1)
    receive(3)
    pre_scores(0, query, keys, raw)
    gather_core(bias_e, at, 2, g_send_e, g_recv_e, recv_b)
    pre_scores(1, query, keys, raw)
    pre_scores(2, query, keys, raw)
    gather_core(bias_e, at, 3, g_send_e, g_recv_e, recv_b)
    settle(2)
    pre_scores(3, query, keys, raw)
    settle(3)

    def end_step(step, carry):
        block = block_of(at, step)
        blocks = [attention_block(i, block, raw, wide, values, gate) for i in range(ROWS)]
        send_block(at, step, block, blocks, send_b, recv_b, to_slots, x_send.at[1, step], x_recv.at[1, step])
        return carry

    lax.fori_loop(0, 4, end_step, 0)
    gather_drain(at, g_send_s, g_recv_s, recv_a)
    gather_drain(at, g_send_e, g_recv_e, recv_a)
    stores = []
    for step in range(4):
        plane = (z + 4 - STEPS[step]) % 4
        here = pl.ds(pl.multiple_of(plane * 128, 128), 128)
        wait_for(recv_b, 32 if step < 3 else 31, at, x_send.at[1, step], x_recv.at[1, step], False)
        for i, rows in enumerate(from_recv(recv_b, plane, to_rows)):
            update = jnp.dot(rows, out_weight_e[...], preferred_element_type=f32)
            pair[i, here, :] = pair[i, here, :] + update + vec(out_bias_e)
        stores.append(pltpu.make_async_copy(pair.at[:, here], out_hbm.at[:, here], out_sem.at[step]))
        stores[-1].start()
    for trip in range(2):
        for step in range(4):
            wait_for(recv_a, 32 if step < 3 else 31, at, x_send.at[trip, step], x_recv.at[trip, step], True)
    for store in stores:
        store.wait()


def body(*args):
    args = [arg.T if arg.shape == (C, H) else arg for arg in args]
    vmem = pl.BlockSpec(memory_space=pltpu.VMEM)
    slab = (4, 4, 4, 2, 16, N)
    return pl.pallas_call(
        kernel,
        out_shape=jax.ShapeDtypeStruct((ROWS, N, C), f32),
        in_specs=[pl.BlockSpec(memory_space=pl.ANY)] + [vmem] * (len(args) - 1),
        out_specs=pl.BlockSpec(memory_space=pl.ANY),
        scratch_shapes=[
            pltpu.VMEM((ROWS, N, C), f32),
            pltpu.VMEM((ROWS, N, C), bf16),
            pltpu.VMEM((ROWS, N, C), bf16),
            pltpu.VMEM((ROWS, N, C), bf16),
            pltpu.VMEM((ROWS, N, C), bf16),
            pltpu.VMEM((ROWS, N, C), f32),
            pltpu.VMEM((4, H * 128, N), f32),
            pltpu.VMEM((4, ROWS, H * 128, N), f32),
            pltpu.VMEM((512, 512), bf16),
            pltpu.VMEM(slab, bf16),
            pltpu.VMEM(slab, bf16),
            pltpu.VMEM((DEV, 16, C), bf16),
            pltpu.VMEM((DEV, 16, C), bf16),
            pltpu.VMEM((DEV, 16, C), bf16),
            pltpu.VMEM((DEV, 16, C), bf16),
            pltpu.SemaphoreType.DMA((4, 8)),
            pltpu.SemaphoreType.DMA((4, 8)),
            pltpu.SemaphoreType.DMA((4, 8)),
            pltpu.SemaphoreType.DMA((4, 8)),
            pltpu.SemaphoreType.DMA((2, 4)),
            pltpu.SemaphoreType.DMA((2, 4)),
            pltpu.SemaphoreType.DMA((4,)),
            pltpu.SemaphoreType.DMA((4,)),
        ],
        compiler_params=pltpu.CompilerParams(
            collective_id=0, has_side_effects=True, vmem_limit_bytes=56 << 20
        ),
    )(*args)


def solution(mesh):
    rows = P(("rb", "cb"), None, None)
    return jax.shard_map(body, mesh=mesh, in_specs=(rows,) + (P(),) * 14, out_specs=rows, check_vma=False)
```
